256 devices in a mesh: dp: 4 (over y), group: 16 (over z_hi, x), tensor: 4 (over z_lo, core).
Axes of the slice: x: 4, y: 4, z: 8 (z_hi: 4, z_lo: 2; z = z_hi * 2 + z_lo), core: 2. Of those that a mesh axis runs over, the one named last changes fastest.
Arguments:
- queries: bfloat16 [4, 16, 256, 4096], P('dp', 'group', None, 'tensor'), may hold values from -6 to 6
- comp_keys: bfloat16 [4, 16, 256, 512], P('dp', 'group', None, 'tensor'), may hold values from -4 to 4
- comp_values: bfloat16 [4, 16, 256, 512], P('dp', 'group', None, 'tensor'), may hold values from -4 to 4
- prompt_keys: bfloat16 [4, 2048, 512], P('dp', 'group', 'tensor'), may hold values from -6 to 6
- prompt_values: bfloat16 [4, 2048, 512], P('dp', 'group', 'tensor'), may hold values from -4 to 4
- out_weight: bfloat16 [4096, 4096], P('tensor'), may hold values from -1.5 to 1.5
- cotangent: bfloat16 [4, 16, 256, 4096], P('dp', 'group', None, 'tensor'), may hold values from -5 to 5
- lengths: int32 [4, 16], P('dp', 'group'), may hold values from 1 to 256, 1216 in all within a row
Outputs:
- output: bfloat16 [4, 16, 256, 4096], P('dp', 'group', None, 'tensor')
- query_grad: bfloat16 [4, 16, 256, 4096], P('dp', 'group', None, 'tensor')
- comp_key_grad: bfloat16 [4, 16, 256, 512], P('dp', 'group', None, 'tensor')
- comp_value_grad: bfloat16 [4, 16, 256, 512], P('dp', 'group', None, 'tensor')
- prompt_key_grad: bfloat16 [4, 2048, 512], P('dp', 'group', 'tensor')
- prompt_value_grad: bfloat16 [4, 2048, 512], P('dp', 'group', 'tensor')
The draws below stay inside these ranges and needn't reach their ends.
Inputs may be any that keep to these rules, and one draw needn't show every extreme that they name: Each prompt's 16 lengths sum to 1216, and the longest of them is exactly 256.
All inputs are finite; a program needn't handle non-finite values. No bound on the sum of `lengths` on one device may be relied on, other than what follows from the above.
Results may differ from the reference program's by a relative error of at most 0.025.
Values may be sent and summed in bfloat16 or wider, within the bound.
No kernel may reach another device: no remote copies, remote signals or barrier semaphores. Data moves between devices by JAX's collectives and lax.ppermute only.
A program may use at most 64 MiB of HBM per device.

```python
import math
import jax
import jax.numpy as jnp
import numpy as np
from jax import lax

D = 4096
HEADS = 32
KV = 4
HD = 128
CMAX = 256
PROMPT = 2048
N_DP = 4
N_GROUP = 16
N_TENSOR = 4


def draw_queries(key, part):
    key = jax.random.fold_in(key, 11)
    full_shape = (N_DP, N_GROUP, CMAX, HEADS, HD)
    values_base = jnp.clip(jax.random.normal(key, full_shape, jnp.float32), -4.0, 4.0)
    return values_base.reshape(N_DP, N_GROUP, CMAX, HEADS * HD).astype(jnp.bfloat16)


def draw_prompt_keys(key, part):
    key = jax.random.fold_in(key, 12)
    full_shape = (N_DP, PROMPT, KV, HD)
    values_base = jnp.clip(jax.random.normal(key, full_shape, jnp.float32), -4.0, 4.0)
    return values_base.reshape(N_DP, PROMPT, KV * HD).astype(jnp.bfloat16)


def block_levels(own_key, shape, shards, low, high):
    level = 1.0
    for position, parts in shards:
        steps = jax.random.uniform(jax.random.fold_in(jax.random.fold_in(own_key, 6), position), (parts,), jnp.float32, low / len(shards), high / len(shards))
        level = level * jnp.repeat(jnp.exp(steps), shape[position] // parts).reshape((-1,) + (1,) * (len(shape) - 1 - position))
    return level


def profile(number_of, total, limit, skew):
    loads = [(1 << 20) // math.isqrt(standing ** skew) + 1 for standing in range(2, number_of + 1)]
    rest, given = total - limit - (number_of - 1), [1] * (number_of - 1)
    while rest > 0:
        free = [i for i in range(number_of - 1) if given[i] < limit]
        mass, left = sum([loads[i] for i in free]), rest
        for i in free:
            extra = min(limit - given[i], max(1, left * loads[i] // mass), rest)
            given[i] = given[i] + extra
            rest = rest - extra
    return np.array([limit] + given)


def ragged(own_key, amount, total, limit, lean):
    if amount == 2:
        one = jax.random.randint(own_key, (), max(1, total - limit), min(limit, total - 1) + 1)
        return jnp.stack([one, total - one])
    sizes = jnp.asarray(profile(amount, total, limit, lean), jnp.int32)
    couples = (amount - 1) // 2
    giver, taker = sizes[1:1 + 2 * couples:2], sizes[2:2 + 2 * couples:2]
    margin = jnp.minimum(giver - 1, limit - taker)
    moved = jax.random.randint(jax.random.fold_in(own_key, 1), (couples,), 0, 1 << 20) % (margin + 1)
    sizes = sizes.at[1:1 + 2 * couples:2].set(giver - moved).at[2:2 + 2 * couples:2].set(taker + moved)
    return sizes[jax.random.permutation(jax.random.fold_in(own_key, 2), amount)]


def normal_values(rng, dims, width, most, split=(), kind=jnp.bfloat16):
    loudness = block_levels(rng, dims, split, -0.22, 0.18) if split else 1.0
    entries = jax.random.normal(rng, dims, jnp.float32) * width * loudness
    return jnp.minimum(jnp.maximum(entries, -most), most).astype(kind)


def setup_inputs(seed: int = 0) -> dict:
    keys = jax.random.split(jax.random.key(seed), 9)
    return {
        "queries": draw_queries(jax.random.fold_in(keys[8], 71), 0),
        "comp_keys": normal_values(keys[1], (N_DP, N_GROUP, CMAX, KV * HD), 1.0, 4.0, ((0, 4), (1, 16), (3, 4))),
        "comp_values": normal_values(keys[2], (N_DP, N_GROUP, CMAX, KV * HD), 1.0, 4.0, ((0, 4), (1, 16), (3, 4))),
        "prompt_keys": draw_prompt_keys(jax.random.fold_in(keys[8], 71), 0),
        "prompt_values": normal_values(keys[4], (N_DP, PROMPT, KV * HD), 1.0, 4.0, ((0, 4), (1, 16), (2, 4))),
        "out_weight": normal_values(keys[5], (HEADS * HD, D), (max(HEADS * HD // 256, 1)) ** -0.5, 1.5, ((0, 4),)),
        "cotangent": normal_values(keys[6], (N_DP, N_GROUP, CMAX, D), 1.0, 5.0, ((0, 4), (1, 16), (3, 4))),
        "lengths": jax.vmap(lambda own: ragged(own, N_GROUP, CMAX + (N_GROUP - 1) * (CMAX // 4), CMAX, 2))(jax.random.split(keys[7], N_DP)).reshape((N_DP, N_GROUP)).astype(jnp.int32),
    }


NEG_FILL = -1e30


def block_pass(query_rows, dout_rows, row_ids, length, all_keys, all_values, prompt_len):
    score_scale = query_rows.shape[-1] ** -0.5
    query_wide = query_rows.astype(jnp.float32)
    dout_wide = dout_rows.astype(jnp.float32)
    keys_wide = all_keys.astype(jnp.float32)
    values_wide = all_values.astype(jnp.float32)
    scores = jnp.einsum("ikgd,jkd->kgij", query_wide, keys_wide) * score_scale
    key_index = jnp.arange(all_keys.shape[0], dtype=jnp.int32)
    live_rows = row_ids < length
    allowed = (key_index[None, :] < prompt_len) | (key_index[None, :] - prompt_len <= row_ids[:, None])
    allowed = allowed & live_rows[:, None]
    masked = jnp.where(allowed, scores, NEG_FILL)
    top_score = jnp.max(masked, axis=-1, keepdims=True)
    expo = jnp.where(allowed, jnp.exp(masked - top_score), 0.0)
    normer = jnp.sum(expo, axis=-1, keepdims=True)
    normer = jnp.where(live_rows[:, None], normer, 1.0)
    attn_weights = expo / normer
    weights_low = attn_weights.astype(jnp.bfloat16)
    low_wide = weights_low.astype(jnp.float32)
    mixed_out = jnp.einsum("kgij,jkd->ikgd", low_wide, values_wide).astype(jnp.bfloat16)
    dprob = jnp.einsum("ikgd,jkd->kgij", dout_wide, values_wide)
    row_delta = jnp.sum(attn_weights * dprob, axis=-1, keepdims=True)
    dscore = (attn_weights * (dprob - row_delta) * score_scale).astype(jnp.bfloat16)
    dscore_wide = dscore.astype(jnp.float32)
    dquery = jnp.einsum("kgij,jkd->ikgd", dscore_wide, keys_wide).astype(jnp.bfloat16)
    dkeys = jnp.einsum("kgij,ikgd->jkd", dscore_wide, query_wide)
    dvalues = jnp.einsum("kgij,ikgd->jkd", low_wide, dout_wide)
    return mixed_out, dquery, dkeys, dvalues


def reference(queries, comp_keys, comp_values, prompt_keys, prompt_values, out_weight, cotangent, lengths):
    per_group = HEADS // KV
    tensor_cols = HEADS * HD // N_TENSOR

    def one_prompt(inputs):
        query_set, ckey_set, cval_set, pkey_one, pval_one, cot_set, length_set = inputs

        def one_comp(sums, items):
            query_one, ckey_one, cval_one, cot_one, length = items
            dout = jnp.dot(cot_one, out_weight.T, preferred_element_type=jnp.float32).astype(jnp.bfloat16)
            all_keys = jnp.concatenate([pkey_one, ckey_one], 0).reshape(-1, KV, HD)
            all_values = jnp.concatenate([pval_one, cval_one], 0).reshape(-1, KV, HD)
            row_ids = jnp.arange(CMAX, dtype=jnp.int32)
            mixed, dquery, dkeys, dvalues = block_pass(
                query_one.reshape(CMAX, KV, per_group, HD), dout.reshape(CMAX, KV, per_group, HD),
                row_ids, length, all_keys, all_values, PROMPT)
            mixed_flat = mixed.reshape(CMAX, HEADS * HD)
            summed = jnp.zeros((CMAX, D), jnp.float32)
            for tensor_rank in range(N_TENSOR):
                lower = tensor_rank * tensor_cols
                partial_term = jnp.dot(mixed_flat[:, lower:lower + tensor_cols], out_weight[lower:lower + tensor_cols],
                                       preferred_element_type=jnp.float32).astype(jnp.bfloat16)
                summed = summed + lax.optimization_barrier(partial_term).astype(jnp.float32)
            results = (summed.astype(jnp.bfloat16), dquery.reshape(CMAX, HEADS * HD),
                       dkeys[PROMPT:].reshape(CMAX, KV * HD).astype(jnp.bfloat16),
                       dvalues[PROMPT:].reshape(CMAX, KV * HD).astype(jnp.bfloat16))
            sums = (sums[0] + dkeys[:PROMPT].reshape(PROMPT, KV * HD), sums[1] + dvalues[:PROMPT].reshape(PROMPT, KV * HD))
            return sums, results

        zero_grads = jnp.zeros((PROMPT, KV * HD), jnp.float32)
        sums, results = lax.scan(one_comp, (zero_grads, zero_grads), (query_set, ckey_set, cval_set, cot_set, length_set))
        return results + (sums[0].astype(jnp.bfloat16), sums[1].astype(jnp.bfloat16))

    stacked = lax.map(one_prompt, (queries, comp_keys, comp_values, prompt_keys, prompt_values, cotangent, lengths))
    return (stacked[0], stacked[1], stacked[2], stacked[3], stacked[4], stacked[5])
```

```python
import functools

import jax
import jax.numpy as jnp
from jax import lax
from jax.experimental import pallas as pl
from jax.experimental.pallas import tpu as pltpu
from jax.sharding import PartitionSpec as P

HD = 128
HEADS = 8
SLOTS = 256
NEG_FILL = -1e30
LOG2E = 1.4426950408889634
SCALE = HD**-0.5
F32 = jnp.float32
BF16 = jnp.bfloat16
VMEM_LIMIT = 48 * 1024 * 1024


def dot_nn(a, b):
    return lax.dot_general(a, b, (((1,), (0,)), ((), ())), preferred_element_type=F32)


def dot_nt(a, b):
    return lax.dot_general(a, b, (((1,), (1,)), ((), ())), preferred_element_type=F32)


def attend(q, tables, turned, causal, weights):
    scores = []
    for table, masked in zip(tables, causal):
        s = dot_nt(table[:, :HD], q) * (SCALE * LOG2E)
        if masked:
            key = lax.broadcasted_iota(jnp.int32, s.shape, 0)
            token = lax.broadcasted_iota(jnp.int32, s.shape, 1)
            s = jnp.where(key <= token, s, NEG_FILL)
        scores.append(s)
    top = functools.reduce(jnp.maximum, [jnp.max(s, axis=0, keepdims=True) for s in scores])
    total, acc = 0.0, 0.0
    for s, vt, w in zip(scores, turned, weights):
        p = jnp.exp2(s - top)
        total = total + jnp.sum(p, axis=0, keepdims=True)
        low = p.astype(BF16)
        w[0] = low
        acc = acc + dot_nn(vt[...], low)
    return top, total, acc


def turn(step, tables, turned, low):
    @pl.when(step == 0)
    def _():
        for table, t in zip(tables, turned):
            t[...] = table[:, low : low + HD].T


def fwd_kernel(count, causal, *refs):
    q = refs[0]
    tables = refs[1 : 1 + count]
    weights = refs[1 + count : 1 + 2 * count]
    top_ref, total_ref, acc_ref = refs[1 + 2 * count : 4 + 2 * count]
    turned = refs[4 + 2 * count :]
    turn(pl.program_id(0), tables, turned, HD)
    top, total, acc = attend(q[...], tables, turned, causal, weights)
    top_ref[0], total_ref[0], acc_ref[...] = top, total, acc


def merge_kernel(count, earlier, *refs):
    length, q, dout = refs[:3]
    tables = refs[3 : 3 + count]
    at = 3 + count
    old = [refs[at + 3 * i : at + 3 * i + 3] for i in range(earlier)]
    at += 3 * earlier
    weights = refs[at : at + count]
    at += count
    alphas = refs[at : at + earlier + 1]
    delta_ref, mixed_ref = refs[at + earlier + 1 : at + earlier + 3]
    turned = refs[at + earlier + 3 :]
    turn(pl.program_id(0), tables, turned, HD)
    parts = [(t[0], l[0], a[...]) for t, l, a in old]
    parts.append(attend(q[...], tables, turned, (False,) * count, weights))
    top = functools.reduce(jnp.maximum, [t for t, _, _ in parts])
    factors = [jnp.exp2(t - top) for t, _, _ in parts]
    total = sum(f * l for f, (_, l, _) in zip(factors, parts))
    live = lax.broadcasted_iota(jnp.int32, top.shape, 1) < length[0, 0]
    inverse = jnp.where(live, 1.0 / total, 0.0)
    mixed = 0.0
    for f, (_, _, acc), alpha in zip(factors, parts, alphas):
        alpha[0] = f * inverse
        mixed = mixed + (f * inverse) * acc
    delta_ref[0] = jnp.sum(mixed * dout[...].astype(F32), axis=0, keepdims=True)
    mixed_ref[...] = mixed.astype(BF16)


def bwd_kernel(count, first, last, *refs):
    q, dout, alpha, delta = refs[:4]
    tables = refs[4 : 4 + count]
    weights = refs[4 + count : 4 + 2 * count]
    at = 4 + 2 * count
    if not first:
        dq_in = refs[at]
        at += 1
    grads = refs[at : at + count]
    dq_ref = refs[at + count]
    turned = refs[at + count + 1 : at + 2 * count + 1]
    sums = refs[at + 2 * count + 1 :]
    step = pl.program_id(0)
    turn(step, tables, turned, 0)

    @pl.when(step == 0)
    def _():
        for s in sums:
            s[...] = jnp.zeros_like(s)

    da = (dout[...].astype(F32) * alpha[0]).astype(BF16)
    shift = delta[0] * alpha[0]
    dq = 0.0 if first else dq_in[...]
    for table, w, kt, s in zip(tables, weights, turned, sums):
        p = w[0]
        dp = dot_nn(table[:, HD:], da)
        ds = (p.astype(F32) * (dp - shift)).astype(BF16)
        s[:, HD:] += dot_nt(p, da)
        s[:, :HD] += dot_nn(ds, q[...])
        dq = dq + dot_nn(kt[...], ds)
    if last:
        dq_ref[...] = (dq * SCALE).T.astype(dq_ref.dtype)
    else:
        dq_ref[...] = dq

    @pl.when(step == HEADS - 1)
    def _():
        for s, g in zip(sums, grads):
            g[:, :HD] = (s[:, :HD] * SCALE).astype(g.dtype)
            g[:, HD:] = s[:, HD:].astype(g.dtype)


Q_SPEC = pl.BlockSpec((SLOTS, HD), lambda h: (0, h))
T_SPEC = pl.BlockSpec((HD, SLOTS), lambda h: (h, 0))
STAT_SPEC = pl.BlockSpec((1, 1, SLOTS), lambda h: (h, 0, 0))
STAT = jax.ShapeDtypeStruct((HEADS, 1, SLOTS), F32)
WIDE = jax.ShapeDtypeStruct((HEADS * HD, SLOTS), F32)
PARAMS = dict(compiler_params=pltpu.CompilerParams(vmem_limit_bytes=VMEM_LIMIT), grid=(HEADS,))


def whole(table):
    return pl.BlockSpec(table.shape, lambda h: (0, 0))


def weight_specs(tables):
    specs = [pl.BlockSpec((1, t.shape[0], SLOTS), lambda h: (h, 0, 0)) for t in tables]
    shapes = [jax.ShapeDtypeStruct((HEADS, t.shape[0], SLOTS), BF16) for t in tables]
    return specs, shapes


def cost(tables, dots):
    rows = sum(t.shape[0] for t in tables)
    area = rows * SLOTS * HEADS
    return pl.CostEstimate(
        flops=4 * dots * area * HD, bytes_accessed=2 * area + 4 * 1024 * 1024, transcendentals=area
    )


def forward(q, tables, causal):
    specs, shapes = weight_specs(tables)
    n = len(tables)
    out = pl.pallas_call(
        functools.partial(fwd_kernel, n, causal),
        in_specs=[Q_SPEC] + [whole(t) for t in tables],
        out_specs=specs + [STAT_SPEC, STAT_SPEC, T_SPEC],
        out_shape=shapes + [STAT, STAT, WIDE],
        scratch_shapes=[pltpu.VMEM((HD, t.shape[0]), BF16) for t in tables],
        cost_estimate=cost(tables, 2),
        name="forward",
        **PARAMS,
    )(q, *tables)
    return out[:n], out[n:]


def forward_merge(length, q, dout, tables, old):
    specs, shapes = weight_specs(tables)
    n = len(tables)
    e = len(old)
    out = pl.pallas_call(
        functools.partial(merge_kernel, n, e),
        in_specs=[pl.BlockSpec(memory_space=pltpu.SMEM), Q_SPEC, T_SPEC]
        + [whole(t) for t in tables]
        + [STAT_SPEC, STAT_SPEC, T_SPEC] * e,
        out_specs=specs + [STAT_SPEC] * (e + 2) + [T_SPEC],
        out_shape=shapes + [STAT] * (e + 2) + [jax.ShapeDtypeStruct((HEADS * HD, SLOTS), BF16)],
        scratch_shapes=[pltpu.VMEM((HD, t.shape[0]), BF16) for t in tables],
        cost_estimate=cost(tables, 2),
        name="forward_merge",
        **PARAMS,
    )(length, q, dout, *tables, *[x for part in old for x in part])
    return out[:n], out[n : n + e + 1], out[n + e + 1], out[n + e + 2]


def backward(q, dout, alpha, delta, tables, weights, kinds, dq, last):
    specs, _ = weight_specs(tables)
    n = len(tables)
    out = pl.pallas_call(
        functools.partial(bwd_kernel, n, dq is None, last),
        in_specs=[Q_SPEC, T_SPEC, STAT_SPEC, STAT_SPEC]
        + [whole(t) for t in tables]
        + specs
        + ([] if dq is None else [T_SPEC]),
        out_specs=[whole(t) for t in tables] + [Q_SPEC if last else T_SPEC],
        out_shape=[jax.ShapeDtypeStruct(t.shape, k) for t, k in zip(tables, kinds)]
        + [jax.ShapeDtypeStruct((SLOTS, HEADS * HD), BF16) if last else WIDE],
        scratch_shapes=[pltpu.VMEM((HD, t.shape[0]), BF16) for t in tables]
        + [pltpu.VMEM(t.shape, F32) for t in tables],
        cost_estimate=cost(tables, 4),
        name="backward",
        **PARAMS,
    )(q, dout, alpha, delta, *tables, *weights, *([] if dq is None else [dq]))
    return out[:n], out[n]


def group_shift(dz, dx):
    return [(z * 4 + x, (z + dz) % 4 * 4 + (x + dx) % 4) for z in range(4) for x in range(4)]


def tensor_flip(bits):
    return [(t, t ^ bits) for t in range(4)]


def per_device(
    queries, comp_keys, comp_values, prompt_keys, prompt_values, out_weight, cotangent, lengths
):
    q = queries[0, 0]
    cot = cotangent[0, 0]

    def over_z(a, s):
        return lax.ppermute(a, "group", group_shift(s, 0))

    def over_x(a, s):
        return lax.ppermute(a, "group", group_shift(0, s))

    def to_core(a):
        return lax.ppermute(a, "tensor", tensor_flip(1))

    def to_chip(a):
        return lax.ppermute(a, "tensor", tensor_flip(2))

    own = jnp.concatenate([prompt_keys[0], prompt_values[0]], axis=1)
    comp = jnp.concatenate([comp_keys[0, 0], comp_values[0, 0]], axis=1)
    chunk0 = jnp.concatenate([own] + [over_z(own, s) for s in (1, 3, 2)], axis=0)
    chunk1, chunk3, chunk2 = [over_x(chunk0, s) for s in (1, 3, 2)]

    me = lax.axis_index("tensor")

    def columns(bits):
        return lax.dynamic_slice_in_dim(out_weight, (me ^ bits) * 1024, 1024, 1)

    cot_chip = to_chip(cot)
    cot_core = to_core(cot)
    cot_diag = to_core(cot_chip)
    dout = sum(
        dot_nt(columns(bits), part)
        for bits, part in ((0, cot), (1, cot_core), (2, cot_chip), (3, cot_diag))
    ).astype(BF16)

    w0, part0 = forward(q, [chunk0, comp], (False, True))
    w13, part13 = forward(q, [chunk1, chunk3], (False, False))
    w2, (alpha0, alpha13, alpha2), delta, mixed = forward_merge(
        lengths, q, dout, [chunk2], [part0, part13]
    )

    (g2,), dq = backward(q, dout, alpha2, delta, [chunk2], w2, (BF16,), None, False)
    (g1, g3), dq = backward(q, dout, alpha13, delta, [chunk1, chunk3], w13, (BF16, BF16), dq, False)

    def partial_out(bits):
        block = lax.dot_general(
            mixed, columns(bits), (((0,), (0,)), ((), ())), preferred_element_type=F32
        )
        return block.astype(BF16)

    other = to_core(jnp.concatenate([partial_out(1), partial_out(3)], axis=0))
    pair_mine = partial_out(0).astype(F32) + other[:SLOTS].astype(F32)
    pair_far = partial_out(2).astype(F32) + other[SLOTS:].astype(F32)
    far = to_chip(pair_far.astype(BF16))
    output = (pair_mine + far.astype(F32)).astype(BF16)

    (g0, gcomp), dq = backward(q, dout, alpha0, delta, [chunk0, comp], w0, (F32, BF16), dq, True)

    back2, back1, back3 = over_x(g2, -2), over_x(g1, -1), over_x(g3, -3)
    rows = g0 + back2.astype(F32) + back1.astype(F32) + back3.astype(F32)
    n = own.shape[0]
    sent = rows.astype(BF16)
    total = rows[:n]
    for i, s in enumerate((1, 3, 2)):
        total = total + over_z(sent[(i + 1) * n : (i + 2) * n], -s).astype(F32)
    total = total.astype(BF16)
    return (
        output[None, None],
        dq[None, None],
        gcomp[None, None, :, :HD],
        gcomp[None, None, :, HD:],
        total[None, :, :HD],
        total[None, :, HD:],
    )


def solution(mesh):
    wide = P("dp", "group", None, "tensor")
    rows = P("dp", "group", "tensor")
    return jax.shard_map(
        per_device,
        mesh=mesh,
        in_specs=(wide, wide, wide, rows, rows, P("tensor", None), wide, P("dp", "group")),
        out_specs=(wide, wide, wide, wide, rows, rows),
        check_vma=False,
    )
```

```python
import functools

import jax
import jax.numpy as jnp
from jax import lax
from jax.experimental import pallas as pl
from jax.experimental.pallas import tpu as pltpu
from jax.sharding import PartitionSpec as P

HD = 128
HEADS = 8
SLOTS = 256
NEG_FILL = -1e30
LOG2E = 1.4426950408889634
SCALE = HD**-0.5
F32 = jnp.float32
BF16 = jnp.bfloat16


def dot_nn(a, b):
    return lax.dot_general(a, b, (((1,), (0,)), ((), ())), preferred_element_type=F32)


def dot_nt(a, b):
    return lax.dot_general(a, b, (((1,), (1,)), ((), ())), preferred_element_type=F32)


def span(i):
    return slice(i * HD, (i + 1) * HD)


def attend(q, tables, causal, weights, scores, turned):
    for table, t in zip(tables, turned):
        t[...] = table[:, HD:].T
    for i in range(HEADS):
        for table, masked, score in zip(tables, causal, scores):
            s = dot_nt(table[:, :HD], q[:, span(i)]) * (SCALE * LOG2E)
            if masked:
                key = lax.broadcasted_iota(jnp.int32, s.shape, 0)
                token = lax.broadcasted_iota(jnp.int32, s.shape, 1)
                s = jnp.where(key <= token, s, NEG_FILL)
            score[i] = s
    stats = []
    for i in range(HEADS):
        top = functools.reduce(
            jnp.maximum, [jnp.max(score[i], axis=0, keepdims=True) for score in scores]
        )
        total = 0.0
        for score, w in zip(scores, weights):
            p = jnp.exp2(score[i] - top)
            total = total + jnp.sum(p, axis=0, keepdims=True)
            w[i] = p.astype(BF16)
        stats.append((top, total))
    return stats


def mix(i, weights, turned):
    return sum(dot_nn(t[...], w[i]) for t, w in zip(turned, weights))


def fwd_kernel(count, causal, *refs):
    q = refs[0]
    tables = refs[1 : 1 + count]
    weights = refs[1 + count : 1 + 2 * count]
    top_ref, total_ref, acc_ref = refs[1 + 2 * count : 4 + 2 * count]
    scores = refs[4 + 2 * count : 4 + 3 * count]
    turned = refs[4 + 3 * count :]
    stats = attend(q, tables, causal, weights, scores, turned)
    for i in range(HEADS):
        top_ref[i], total_ref[i] = stats[i]
        acc_ref[span(i), :] = mix(i, weights, turned)


def merge_kernel(count, earlier, *refs):
    length, q, dout = refs[:3]
    tables = refs[3 : 3 + count]
    at = 3 + count
    old = [refs[at + 3 * i : at + 3 * i + 3] for i in range(earlier)]
    at += 3 * earlier
    weights = refs[at : at + count]
    at += count
    alphas = refs[at : at + earlier + 1]
    delta_ref, mixed_ref = refs[at + earlier + 1 : at + earlier + 3]
    at += earlier + 3
    scores = refs[at : at + count]
    turned = refs[at + count :]
    stats = attend(q, tables, (False,) * count, weights, scores, turned)
    for i in range(HEADS):
        parts = [(t[i], l[i], a[span(i), :]) for t, l, a in old]
        parts.append((*stats[i], mix(i, weights, turned)))
        top = functools.reduce(jnp.maximum, [t for t, _, _ in parts])
        factors = [jnp.exp2(t - top) for t, _, _ in parts]
        total = sum(f * l for f, (_, l, _) in zip(factors, parts))
        live = lax.broadcasted_iota(jnp.int32, top.shape, 1) < length[0, 0]
        inverse = jnp.where(live, 1.0 / total, 0.0)
        mixed = 0.0
        for f, (_, _, acc), alpha in zip(factors, parts, alphas):
            alpha[i] = f * inverse
            mixed = mixed + (f * inverse) * acc
        delta_ref[i] = jnp.sum(mixed * dout[span(i), :].astype(F32), axis=0, keepdims=True)
        mixed_ref[span(i), :] = mixed.astype(BF16)


def bwd_kernel(count, first, last, *refs):
    q, dout, alpha, delta = refs[:4]
    tables = refs[4 : 4 + count]
    weights = refs[4 + count : 4 + 2 * count]
    at = 4 + 2 * count
    if not first:
        dq_in = refs[at]
        at += 1
    grads = refs[at : at + count]
    dq_ref = refs[at + count]
    turned = refs[at + count + 1 : at + 2 * count + 1]
    sums = refs[at + 2 * count + 1 :]
    for table, t in zip(tables, turned):
        t[...] = table[:, :HD].T
    for s in sums:
        s[...] = jnp.zeros_like(s)
    for i in range(HEADS):
        da = (dout[span(i), :].astype(F32) * alpha[i]).astype(BF16)
        shift = delta[i] * alpha[i]
        dq = 0.0 if first else dq_in[span(i), :]
        for table, w, kt, s in zip(tables, weights, turned, sums):
            p = w[i]
            dp = dot_nn(table[:, HD:], da)
            ds = (p.astype(F32) * (dp - shift)).astype(BF16)
            s[:, HD:] += dot_nt(p, da)
            s[:, :HD] += dot_nn(ds, q[:, span(i)])
            dq = dq + dot_nn(kt[...], ds)
        if last:
            dq_ref[:, span(i)] = (dq * SCALE).T.astype(dq_ref.dtype)
        else:
            dq_ref[span(i), :] = dq
    for s, g in zip(sums, grads):
        g[:, :HD] = (s[:, :HD] * SCALE).astype(g.dtype)
        g[:, HD:] = s[:, HD:].astype(g.dtype)


IN_VMEM = pl.BlockSpec(memory_space=pltpu.VMEM)
STAT = pltpu.VMEM((HEADS, 1, SLOTS), F32)
WIDE = pltpu.VMEM((HEADS * HD, SLOTS), F32)
PARAMS = pltpu.CompilerParams(vmem_limit_bytes=20 * 1024 * 1024)


def call(kernel, name, operands, shapes, scratch, cost, specs=None):
    return pl.pallas_call(
        kernel,
        in_specs=specs or [IN_VMEM] * len(operands),
        out_specs=[IN_VMEM] * len(shapes),
        out_shape=shapes,
        scratch_shapes=scratch,
        cost_estimate=cost,
        compiler_params=PARAMS,
        name=name,
    )(*operands)


def weight_shapes(tables):
    return [pltpu.VMEM((HEADS, t.shape[0], SLOTS), BF16) for t in tables]


def score_shapes(tables):
    return [pltpu.VMEM((HEADS, t.shape[0], SLOTS), F32) for t in tables]


def turned_shapes(tables):
    return [pltpu.VMEM((HD, t.shape[0]), BF16) for t in tables]


def cost(tables, dots):
    rows = sum(t.shape[0] for t in tables)
    area = rows * SLOTS * HEADS
    return pl.CostEstimate(flops=dots * area * HD // 16, bytes_accessed=area // 16, transcendentals=0)


def forward(q, tables, causal):
    n = len(tables)
    out = call(
        functools.partial(fwd_kernel, n, causal),
        "forward",
        [q, *tables],
        weight_shapes(tables) + [STAT, STAT, WIDE],
        score_shapes(tables) + turned_shapes(tables),
        cost(tables, 2),
    )
    return out[:n], out[n:]


def forward_merge(length, q, dout, tables, old):
    n = len(tables)
    e = len(old)
    operands = [length, q, dout, *tables, *[x for part in old for x in part]]
    out = call(
        functools.partial(merge_kernel, n, e),
        "forward_merge",
        operands,
        weight_shapes(tables) + [STAT] * (e + 2) + [pltpu.VMEM((HEADS * HD, SLOTS), BF16)],
        score_shapes(tables) + turned_shapes(tables),
        cost(tables, 2),
        [pl.BlockSpec(memory_space=pltpu.SMEM)] + [IN_VMEM] * (len(operands) - 1),
    )
    return out[:n], out[n : n + e + 1], out[n + e + 1], out[n + e + 2]


def backward(q, dout, alpha, delta, tables, weights, kinds, dq, last):
    n = len(tables)
    out = call(
        functools.partial(bwd_kernel, n, dq is None, last),
        "backward",
        [q, dout, alpha, delta, *tables, *weights, *([] if dq is None else [dq])],
        [jax.ShapeDtypeStruct(t.shape, k) for t, k in zip(tables, kinds)]
        + [jax.ShapeDtypeStruct((SLOTS, HEADS * HD), BF16) if last else WIDE],
        turned_shapes(tables) + [pltpu.VMEM(t.shape, F32) for t in tables],
        cost(tables, 4),
    )
    return out[:n], out[n]


def group_shift(dz, dx):
    return [(z * 4 + x, (z + dz) % 4 * 4 + (x + dx) % 4) for z in range(4) for x in range(4)]


def tensor_flip(bits):
    return [(t, t ^ bits) for t in range(4)]


def per_device(
    queries, comp_keys, comp_values, prompt_keys, prompt_values, out_weight, cotangent, lengths
):
    q = queries[0, 0]
    cot = cotangent[0, 0]

    def over_z(a, s):
        return lax.ppermute(a, "group", group_shift(s, 0))

    def over_x(a, s):
        return lax.ppermute(a, "group", group_shift(0, s))

    def to_core(a):
        return lax.ppermute(a, "tensor", tensor_flip(1))

    def to_chip(a):
        return lax.ppermute(a, "tensor", tensor_flip(2))

    own = jnp.concatenate([prompt_keys[0], prompt_values[0]], axis=1)
    comp = jnp.concatenate([comp_keys[0, 0], comp_values[0, 0]], axis=1)
    gathered = [over_z(own, s) for s in (1, 3, 2)]
    chunk0 = jnp.concatenate([own, *gathered], axis=0)
    chunk0, cot = lax.optimization_barrier((chunk0, cot))
    chunk1, chunk3, chunk2 = [over_x(chunk0, s) for s in (1, 3, 2)]

    me = lax.axis_index("tensor")

    def columns(bits):
        return lax.dynamic_slice_in_dim(out_weight, (me ^ bits) * 1024, 1024, 1)

    cot_chip = to_chip(cot)
    cot_core = to_core(cot)
    cot_diag = to_core(cot_chip)
    dout = sum(
        dot_nt(columns(bits), part)
        for bits, part in ((0, cot), (1, cot_core), (2, cot_chip), (3, cot_diag))
    ).astype(BF16)

    w0, part0 = forward(q, [chunk0, comp], (False, True))
    w13, part13 = forward(q, [chunk1, chunk3], (False, False))
    w2, (alpha0, alpha13, alpha2), delta, mixed = forward_merge(
        lengths, q, dout, [chunk2], [part0, part13]
    )

    (g2,), dq = backward(q, dout, alpha2, delta, [chunk2], w2, (BF16,), None, False)
    def partial_out(bits):
        block = lax.dot_general(
            mixed, columns(bits), (((0,), (0,)), ((), ())), preferred_element_type=F32
        )
        return block.astype(BF16)

    other = to_core(jnp.concatenate([partial_out(1), partial_out(3)], axis=0))
    pair_mine = partial_out(0).astype(F32) + other[:SLOTS].astype(F32)
    pair_far = partial_out(2).astype(F32) + other[SLOTS:].astype(F32)
    pair_far, alpha13 = lax.optimization_barrier((pair_far.astype(BF16), alpha13))
    far = to_chip(pair_far)
    (g1,), dq = backward(q, dout, alpha13, delta, [chunk1], w13[:1], (BF16,), dq, False)
    (g3,), dq = backward(q, dout, alpha13, delta, [chunk3], w13[1:], (BF16,), dq, False)

    (g0, gcomp), dq = backward(q, dout, alpha0, delta, [chunk0, comp], w0, (F32, BF16), dq, True)

    back2, back1, back3 = over_x(g2, -2), over_x(g1, -1), over_x(g3, -3)
    rows = g0 + back2.astype(F32) + back1.astype(F32) + back3.astype(F32)
    n = own.shape[0]
    sent, far = lax.optimization_barrier((rows.astype(BF16), far))
    total = rows[:n]
    for i, s in enumerate((1, 3, 2)):
        total = total + over_z(sent[(i + 1) * n : (i + 2) * n], -s).astype(F32)
    total = total.astype(BF16)
    output = (pair_mine + far.astype(F32)).astype(BF16)
    return (
        output[None, None],
        dq[None, None],
        gcomp[None, None, :, :HD],
        gcomp[None, None, :, HD:],
        total[None, :, :HD],
        total[None, :, HD:],
    )


def solution(mesh):
    wide = P("dp", "group", None, "tensor")
    rows = P("dp", "group", "tensor")
    return jax.shard_map(
        per_device,
        mesh=mesh,
        in_specs=(wide, wide, wide, rows, rows, P("tensor", None), wide, P("dp", "group")),
        out_specs=(wide, wide, wide, wide, rows, rows),
        check_vma=False,
    )
```

```python
import functools

import jax
import jax.numpy as jnp
from jax import lax
from jax.experimental import pallas as pl
from jax.experimental.pallas import tpu as pltpu
from jax.sharding import PartitionSpec as P

HD = 128
HEADS = 8
SLOTS = 256
NEG_FILL = -1e30
LOG2E = 1.4426950408889634
SCALE = HD**-0.5
F32 = jnp.float32
BF16 = jnp.bfloat16
FIRST_VMEM = 56


def dot_nn(a, b):
    return lax.dot_general(a, b, (((1,), (0,)), ((), ())), preferred_element_type=F32)


def dot_nt(a, b):
    return lax.dot_general(a, b, (((1,), (1,)), ((), ())), preferred_element_type=F32)


def span(i):
    return slice(i * HD, (i + 1) * HD)


def keys(table):
    return table[0][...] if len(table) == 2 else table[0][:, :HD]


def values(table):
    return table[1][...] if len(table) == 2 else table[0][:, HD:]


def regroup(refs, widths):
    refs = iter(refs)
    return [tuple(next(refs) for _ in range(w)) for w in widths]


def attend(q, tables, causal, weights, scores, turned):
    for table, t in zip(tables, turned):
        t[...] = values(table).T
    for i in range(HEADS):
        for table, masked, score in zip(tables, causal, scores):
            s = dot_nt(keys(table), q[:, span(i)]) * (SCALE * LOG2E)
            if masked:
                key = lax.broadcasted_iota(jnp.int32, s.shape, 0)
                token = lax.broadcasted_iota(jnp.int32, s.shape, 1)
                s = jnp.where(key <= token, s, NEG_FILL)
            score[i] = s
    stats = []
    for i in range(HEADS):
        top = functools.reduce(
            jnp.maximum, [jnp.max(score[i], axis=0, keepdims=True) for score in scores]
        )
        total = 0.0
        for score, w in zip(scores, weights):
            p = jnp.exp2(score[i] - top)
            total = total + jnp.sum(p, axis=0, keepdims=True)
            w[i] = p.astype(BF16)
        stats.append((top, total))
    return stats


def mix(i, weights, turned):
    return sum(dot_nn(t[...], w[i]) for t, w in zip(turned, weights))


def fwd_kernel(widths, causal, *refs):
    count = len(widths)
    q = refs[0]
    at = 1 + sum(widths)
    tables = regroup(refs[1:at], widths)
    weights = refs[at : at + count]
    top_ref, total_ref, acc_ref = refs[at + count : at + count + 3]
    scores = refs[at + count + 3 : at + 2 * count + 3]
    turned = refs[at + 2 * count + 3 :]
    stats = attend(q, tables, causal, weights, scores, turned)
    for i in range(HEADS):
        top_ref[i], total_ref[i] = stats[i]
        acc_ref[span(i), :] = mix(i, weights, turned)


def first_kernel(*refs):
    sources = refs[:3]
    w, top_ref, total_ref, acc_ref = refs[3:7]
    q, key, value = held = refs[7:10]
    score, turned, sems = refs[10:]
    copies = [
        pltpu.make_async_copy(source, target, sems.at[i])
        for i, (source, target) in enumerate(zip(sources, held))
    ]
    for copy in copies:
        copy.start()
    for copy in copies:
        copy.wait()
    stats = attend(q, [(key, value)], (True,), [w], [score], [turned])
    for i in range(HEADS):
        top_ref[i], total_ref[i] = stats[i]
        acc_ref[span(i), :] = mix(i, [w], [turned])


def merge_kernel(count, earlier, *refs):
    length, q, dout = refs[:3]
    tables = [(t,) for t in refs[3 : 3 + count]]
    at = 3 + count
    old = [refs[at + 3 * i : at + 3 * i + 3] for i in range(earlier)]
    at += 3 * earlier
    weights = refs[at : at + count]
    at += count
    alphas = refs[at : at + earlier + 1]
    delta_ref, mixed_ref = refs[at + earlier + 1 : at + earlier + 3]
    at += earlier + 3
    scores = refs[at : at + count]
    turned = refs[at + count :]
    stats = attend(q, tables, (False,) * count, weights, scores, turned)
    for i in range(HEADS):
        parts = [(t[i], l[i], a[span(i), :]) for t, l, a in old]
        parts.append((*stats[i], mix(i, weights, turned)))
        top = functools.reduce(jnp.maximum, [t for t, _, _ in parts])
        factors = [jnp.exp2(t - top) for t, _, _ in parts]
        total = sum(f * l for f, (_, l, _) in zip(factors, parts))
        live = lax.broadcasted_iota(jnp.int32, top.shape, 1) < length[0, 0]
        inverse = jnp.where(live, 1.0 / total, 0.0)
        mixed = 0.0
        for f, (_, _, acc), alpha in zip(factors, parts, alphas):
            alpha[i] = f * inverse
            mixed = mixed + (f * inverse) * acc
        delta_ref[i] = jnp.sum(mixed * dout[span(i), :].astype(F32), axis=0, keepdims=True)
        mixed_ref[span(i), :] = mixed.astype(BF16)


def bwd_kernel(widths, first, last, *refs):
    count = len(widths)
    q, dout, delta = refs[:3]
    alphas = refs[3 : 3 + count]
    at = 3 + count
    tables = regroup(refs[at : at + sum(widths)], widths)
    at += sum(widths)
    weights = refs[at : at + count]
    at += count
    if not first:
        dq_in = refs[at]
        at += 1
    grads = regroup(refs[at : at + sum(widths)], widths)
    at += sum(widths)
    dq_ref = refs[at]
    turned = refs[at + 1 : at + count + 1]
    sums = refs[at + count + 1 :]
    for table, t in zip(tables, turned):
        t[...] = keys(table).T
    for s in sums:
        s[...] = jnp.zeros_like(s)
    for i in range(HEADS):
        dq = 0.0 if first else dq_in[span(i), :]
        for table, alpha, w, kt, s in zip(tables, alphas, weights, turned, sums):
            da = (dout[span(i), :].astype(F32) * alpha[i]).astype(BF16)
            shift = delta[i] * alpha[i]
            p = w[i]
            dp = dot_nn(values(table), da)
            ds = (p.astype(F32) * (dp - shift)).astype(BF16)
            s[:, HD:] += dot_nt(p, da)
            s[:, :HD] += dot_nn(ds, q[:, span(i)])
            dq = dq + dot_nn(kt[...], ds)
        if last:
            dq_ref[:, span(i)] = (dq * SCALE).T.astype(dq_ref.dtype)
        else:
            dq_ref[span(i), :] = dq
    for s, g in zip(sums, grads):
        low, high = s[:, :HD] * SCALE, s[:, HD:]
        if len(g) == 2:
            g[0][...], g[1][...] = low.astype(g[0].dtype), high.astype(g[1].dtype)
        else:
            g[0][:, :HD], g[0][:, HD:] = low.astype(g[0].dtype), high.astype(g[0].dtype)


IN_VMEM = pl.BlockSpec(memory_space=pltpu.VMEM)
STAT = pltpu.VMEM((HEADS, 1, SLOTS), F32)
WIDE = pltpu.VMEM((HEADS * HD, SLOTS), F32)
PARAMS = pltpu.CompilerParams(vmem_limit_bytes=20 * 1024 * 1024)


def call(kernel, name, operands, shapes, scratch, cost, specs=None, params=PARAMS):
    return pl.pallas_call(
        kernel,
        in_specs=specs or [IN_VMEM] * len(operands),
        out_specs=[IN_VMEM] * len(shapes),
        out_shape=shapes,
        scratch_shapes=scratch,
        cost_estimate=cost,
        compiler_params=params,
        name=name,
    )(*operands)


def weight_shapes(tables):
    return [pltpu.VMEM((HEADS, t.shape[0], SLOTS), BF16) for (t, *_) in tables]


def score_shapes(tables):
    return [pltpu.VMEM((HEADS, t.shape[0], SLOTS), F32) for (t, *_) in tables]


def turned_shapes(tables):
    return [pltpu.VMEM((HD, t.shape[0]), BF16) for (t, *_) in tables]


def cost(tables, dots, share=16):
    rows = sum(t[0].shape[0] for t in tables)
    area = rows * SLOTS * HEADS
    return pl.CostEstimate(
        flops=int(dots * area * HD / share), bytes_accessed=area // 16, transcendentals=0
    )


def forward(q, tables, causal, share=16):
    n = len(tables)
    out = call(
        functools.partial(fwd_kernel, [len(t) for t in tables], causal),
        "forward",
        [q, *[x for t in tables for x in t]],
        weight_shapes(tables) + [STAT, STAT, WIDE],
        score_shapes(tables) + turned_shapes(tables),
        cost(tables, 2, share),
    )
    return out[:n], out[n:]


def forward_first(*sources):
    tables = [sources[1:3]]
    out = call(
        first_kernel,
        "forward_first",
        sources,
        weight_shapes(tables)
        + [STAT, STAT, WIDE]
        + [pltpu.VMEM(x.shape, x.dtype) for x in sources],
        score_shapes(tables) + turned_shapes(tables) + [pltpu.SemaphoreType.DMA((3,))],
        cost(tables, 2),
        [pl.BlockSpec(memory_space=pl.ANY)] * 3,
        pltpu.CompilerParams(vmem_limit_bytes=FIRST_VMEM * 1024 * 1024),
    )
    return out[:1], out[1:4], out[4:]


def forward_merge(length, q, dout, tables, old):
    n = len(tables)
    e = len(old)
    operands = [length, q, dout, *[t for (t,) in tables], *[x for part in old for x in part]]
    out = call(
        functools.partial(merge_kernel, n, e),
        "forward_merge",
        operands,
        weight_shapes(tables) + [STAT] * (e + 2) + [pltpu.VMEM((HEADS * HD, SLOTS), BF16)],
        score_shapes(tables) + turned_shapes(tables),
        cost(tables, 2),
        [pl.BlockSpec(memory_space=pltpu.SMEM)] + [IN_VMEM] * (len(operands) - 1),
    )
    return out[:n], out[n : n + e + 1], out[n + e + 1], out[n + e + 2]


def backward(q, dout, delta, alphas, tables, weights, kind, dq, last):
    flat = [x for t in tables for x in t]
    kinds = [kind if len(t) == 1 else BF16 for t in tables for _ in t]
    out = call(
        functools.partial(bwd_kernel, [len(t) for t in tables], dq is None, last),
        "backward",
        [q, dout, delta, *alphas, *flat, *weights, *([] if dq is None else [dq])],
        [jax.ShapeDtypeStruct(t.shape, k) for t, k in zip(flat, kinds)]
        + [jax.ShapeDtypeStruct((SLOTS, HEADS * HD), BF16) if last else WIDE],
        turned_shapes(tables) + [pltpu.VMEM((t[0].shape[0], 2 * HD), F32) for t in tables],
        cost(tables, 4),
    )
    return out[:-1], out[-1]


def group_shift(dz, dx):
    return [(z * 4 + x, (z + dz) % 4 * 4 + (x + dx) % 4) for z in range(4) for x in range(4)]


def tensor_flip(bits):
    return [(t, t ^ bits) for t in range(4)]


def per_device(
    queries, comp_keys, comp_values, prompt_keys, prompt_values, out_weight, cotangent, lengths
):
    q = queries[0, 0]
    cot = cotangent[0, 0]

    def over_z(a, s):
        return lax.ppermute(a, "group", group_shift(s, 0))

    def over_x(a, s):
        return lax.ppermute(a, "group", group_shift(0, s))

    def to_core(a):
        return lax.ppermute(a, "tensor", tensor_flip(1))

    def to_chip(a):
        return lax.ppermute(a, "tensor", tensor_flip(2))

    own = jnp.concatenate([prompt_keys[0], prompt_values[0]], axis=1)
    own, comp_k = lax.optimization_barrier((own, comp_keys[0, 0]))
    wc, partc, (q, comp_k, comp_v) = forward_first(q, comp_k, comp_values[0, 0])
    comp = (comp_k, comp_v)
    (topc, totalc, accc), cot_late = lax.optimization_barrier((partc, cot))
    partc = (topc, totalc, accc)
    chunk0 = jnp.concatenate([own] + [over_z(own, s) for s in (1, 3, 2)], axis=0)
    chunk1, chunk3, chunk2 = [over_x(chunk0, s) for s in (1, 3, 2)]

    me = lax.axis_index("tensor")

    def columns(bits):
        return lax.dynamic_slice_in_dim(out_weight, (me ^ bits) * 1024, 1024, 1)

    cot_core = to_core(cot)
    cot_chip = to_chip(cot_late)
    cot_diag = to_core(cot_chip)
    w0, part0 = forward(q, [(chunk0,)], (False,), 0.02)
    part0, cot = lax.optimization_barrier((part0, cot))
    most = sum(
        dot_nt(columns(bits), part) for bits, part in ((0, cot), (1, cot_core), (2, cot_chip))
    )
    most, chunk1 = lax.optimization_barrier((most, chunk1))
    w13, part13 = forward(q, [(chunk1,), (chunk3,)], (False, False))
    dout = (most + dot_nt(columns(3), cot_diag)).astype(BF16)
    w2, (alphac, alpha0, alpha13, alpha2), delta, mixed = forward_merge(
        lengths, q, dout, [(chunk2,)], [partc, part0, part13]
    )
    (g2,), dq = backward(q, dout, delta, [alpha2], [(chunk2,)], w2, BF16, None, False)

    def partial_out(bits):
        block = lax.dot_general(
            mixed, columns(bits), (((0,), (0,)), ((), ())), preferred_element_type=F32
        )
        return block.astype(BF16)

    other = to_core(jnp.concatenate([partial_out(1), partial_out(3)], axis=0))
    other, dq = lax.optimization_barrier((other, dq))
    pair_mine = partial_out(0).astype(F32) + other[:SLOTS].astype(F32)
    pair_far = partial_out(2).astype(F32) + other[SLOTS:].astype(F32)
    pair_far, alpha13 = lax.optimization_barrier((pair_far.astype(BF16), alpha13))
    far = to_chip(pair_far)
    (g1, g3), dq = backward(
        q, dout, delta, [alpha13, alpha13], [(chunk1,), (chunk3,)], w13, BF16, dq, False
    )
    (g0, gck, gcv), dq = backward(
        q, dout, delta, [alpha0, alphac], [(chunk0,), comp], [*w0, *wc], F32, dq, True
    )

    back2, far = lax.optimization_barrier((over_x(g2, -2), far))
    back1, back3 = over_x(g1, -1), over_x(g3, -3)
    rows = g0 + back2.astype(F32) + back1.astype(F32) + back3.astype(F32)
    n = own.shape[0]
    sent = rows.astype(BF16)
    total = rows[:n]
    for i, s in enumerate((1, 3, 2)):
        total = total + over_z(sent[(i + 1) * n : (i + 2) * n], -s).astype(F32)
    total = total.astype(BF16)
    output = (pair_mine + far.astype(F32)).astype(BF16)
    return (
        output[None, None],
        dq[None, None],
        gck[None, None],
        gcv[None, None],
        total[None, :, :HD],
        total[None, :, HD:],
    )


def solution(mesh):
    wide = P("dp", "group", None, "tensor")
    rows = P("dp", "group", "tensor")
    return jax.shard_map(
        per_device,
        mesh=mesh,
        in_specs=(wide, wide, wide, rows, rows, P("tensor", None), wide, P("dp", "group")),
        out_specs=(wide, wide, wide, wide, rows, rows),
        check_vma=False,
    )
```

```python
import functools

import jax
import jax.numpy as jnp
from jax import lax
from jax.experimental import pallas as pl
from jax.experimental.pallas import tpu as pltpu
from jax.sharding import PartitionSpec as P

HD = 128
HEADS = 8
SLOTS = 256
NEG_FILL = -1e30
LOG2E = 1.4426950408889634
SCALE = HD**-0.5
F32 = jnp.float32
BF16 = jnp.bfloat16
FIRST_VMEM = 56


def dot_nn(a, b):
    return lax.dot_general(a, b, (((1,), (0,)), ((), ())), preferred_element_type=F32)


def dot_nt(a, b):
    return lax.dot_general(a, b, (((1,), (1,)), ((), ())), preferred_element_type=F32)


def span(i):
    return slice(i * HD, (i + 1) * HD)


def wide(i):
    return slice(i * SLOTS, (i + 1) * SLOTS)


def keys(table):
    return table[0][...] if len(table) == 2 else table[0][:, :HD]


def values(table):
    return table[1][...] if len(table) == 2 else table[0][:, HD:]


def regroup(refs, widths):
    refs = iter(refs)
    return [tuple(next(refs) for _ in range(w)) for w in widths]


def attend(q, tables, causal, weights, scores, turned):
    for table, t in zip(tables, turned):
        t[...] = values(table).T
    for i in range(HEADS):
        for table, masked, score in zip(tables, causal, scores):
            s = dot_nt(keys(table), q[:, span(i)]) * (SCALE * LOG2E)
            if masked:
                key = lax.broadcasted_iota(jnp.int32, s.shape, 0)
                token = lax.broadcasted_iota(jnp.int32, s.shape, 1)
                s = jnp.where(key <= token, s, NEG_FILL)
            score[i] = s
    stats = []
    for i in range(HEADS):
        top = functools.reduce(
            jnp.maximum, [jnp.max(score[i], axis=0, keepdims=True) for score in scores]
        )
        total = 0.0
        for score, w in zip(scores, weights):
            p = jnp.exp2(score[i] - top)
            total = total + jnp.sum(p, axis=0, keepdims=True)
            w[:, wide(i)] = p.astype(BF16)
        stats.append((top, total))
    return stats


def mix(i, weights, turned):
    return sum(dot_nn(t[...], w[:, wide(i)]) for t, w in zip(turned, weights))


def fwd_kernel(widths, causal, *refs):
    count = len(widths)
    q = refs[0]
    at = 1 + sum(widths)
    tables = regroup(refs[1:at], widths)
    weights = refs[at : at + count]
    top_ref, total_ref, acc_ref = refs[at + count : at + count + 3]
    scores = refs[at + count + 3 : at + 2 * count + 3]
    turned = refs[at + 2 * count + 3 :]
    stats = attend(q, tables, causal, weights, scores, turned)
    for i in range(HEADS):
        top_ref[i], total_ref[i] = stats[i]
        acc_ref[span(i), :] = mix(i, weights, turned)


def first_kernel(*refs):
    sources = refs[:3]
    w, top_ref, total_ref, acc_ref = refs[3:7]
    q, key, value = held = refs[7:10]
    score, turned, sems = refs[10:]
    copies = [
        pltpu.make_async_copy(source, target, sems.at[i])
        for i, (source, target) in enumerate(zip(sources, held))
    ]
    for copy in copies:
        copy.start()
    for copy in copies:
        copy.wait()
    stats = attend(q, [(key, value)], (True,), [w], [score], [turned])
    for i in range(HEADS):
        top_ref[i], total_ref[i] = stats[i]
        acc_ref[span(i), :] = mix(i, [w], [turned])


def merge_kernel(count, earlier, *refs):
    length, q, dout = refs[:3]
    tables = [(t,) for t in refs[3 : 3 + count]]
    at = 3 + count
    old = [refs[at + 3 * i : at + 3 * i + 3] for i in range(earlier)]
    at += 3 * earlier
    weights = refs[at : at + count]
    at += count
    alphas = refs[at : at + earlier + 1]
    delta_ref, mixed_ref = refs[at + earlier + 1 : at + earlier + 3]
    at += earlier + 3
    scores = refs[at : at + count]
    turned = refs[at + count :]
    stats = attend(q, tables, (False,) * count, weights, scores, turned)
    for i in range(HEADS):
        parts = [(t[i], l[i], a[span(i), :]) for t, l, a in old]
        parts.append((*stats[i], mix(i, weights, turned)))
        top = functools.reduce(jnp.maximum, [t for t, _, _ in parts])
        factors = [jnp.exp2(t - top) for t, _, _ in parts]
        total = sum(f * l for f, (_, l, _) in zip(factors, parts))
        live = lax.broadcasted_iota(jnp.int32, top.shape, 1) < length[0, 0]
        inverse = jnp.where(live, 1.0 / total, 0.0)
        mixed = 0.0
        for f, (_, _, acc), alpha in zip(factors, parts, alphas):
            alpha[i] = f * inverse
            mixed = mixed + (f * inverse) * acc
        delta_ref[i] = jnp.sum(mixed * dout[span(i), :].astype(F32), axis=0, keepdims=True)
        mixed_ref[span(i), :] = mixed.astype(BF16)


def bwd_kernel(widths, first, last, *refs):
    count = len(widths)
    q, dout, delta = refs[:3]
    alphas = refs[3 : 3 + count]
    at = 3 + count
    tables = regroup(refs[at : at + sum(widths)], widths)
    at += sum(widths)
    weights = refs[at : at + count]
    at += count
    if not first:
        dq_in = refs[at]
        at += 1
    grads = regroup(refs[at : at + sum(widths)], widths)
    at += sum(widths)
    dq_ref = refs[at]
    turned = refs[at + 1 : at + count + 1]
    slopes = refs[at + count + 1 : at + 2 * count + 1]
    scaled = refs[at + 2 * count + 1 : at + 3 * count + 1]
    (rows,) = refs[at + 3 * count + 1 :]
    for table, t in zip(tables, turned):
        t[...] = keys(table).T
    for i in range(HEADS):
        rows[wide(i), :] = q[:, span(i)]
        for table, alpha, w, ds, da in zip(tables, alphas, weights, slopes, scaled):
            da[:, wide(i)] = (dout[span(i), :].astype(F32) * alpha[i]).astype(BF16)
            dp = dot_nn(values(table), da[:, wide(i)])
            p = w[:, wide(i)].astype(F32)
            ds[:, wide(i)] = (p * (dp - delta[i] * alpha[i])).astype(BF16)
    for w, ds, da, g in zip(weights, slopes, scaled, grads):
        low, high = dot_nn(ds[...], rows[...]) * SCALE, dot_nt(w[...], da[...])
        if len(g) == 2:
            g[0][...], g[1][...] = low.astype(g[0].dtype), high.astype(g[1].dtype)
        else:
            g[0][:, :HD], g[0][:, HD:] = low.astype(g[0].dtype), high.astype(g[0].dtype)
    for i in range(HEADS):
        dq = sum(dot_nn(kt[...], ds[:, wide(i)]) for kt, ds in zip(turned, slopes))
        if not first:
            dq = dq + dq_in[span(i), :]
        if last:
            dq_ref[:, span(i)] = (dq * SCALE).T.astype(dq_ref.dtype)
        else:
            dq_ref[span(i), :] = dq


IN_VMEM = pl.BlockSpec(memory_space=pltpu.VMEM)
STAT = pltpu.VMEM((HEADS, 1, SLOTS), F32)
WIDE = pltpu.VMEM((HEADS * HD, SLOTS), F32)
PARAMS = pltpu.CompilerParams(vmem_limit_bytes=20 * 1024 * 1024)


def call(kernel, name, operands, shapes, scratch, cost, specs=None, params=PARAMS):
    return pl.pallas_call(
        kernel,
        in_specs=specs or [IN_VMEM] * len(operands),
        out_specs=[IN_VMEM] * len(shapes),
        out_shape=shapes,
        scratch_shapes=scratch,
        cost_estimate=cost,
        compiler_params=params,
        name=name,
    )(*operands)


def weight_shapes(tables):
    return [pltpu.VMEM((t.shape[0], HEADS * SLOTS), BF16) for (t, *_) in tables]


def score_shapes(tables):
    return [pltpu.VMEM((HEADS, t.shape[0], SLOTS), F32) for (t, *_) in tables]


def turned_shapes(tables):
    return [pltpu.VMEM((HD, t.shape[0]), BF16) for (t, *_) in tables]


def cost(tables, dots, share=16):
    rows = sum(t[0].shape[0] for t in tables)
    area = rows * SLOTS * HEADS
    return pl.CostEstimate(
        flops=int(dots * area * HD / share), bytes_accessed=area // 16, transcendentals=0
    )


def forward(q, tables, causal, share=16):
    n = len(tables)
    out = call(
        functools.partial(fwd_kernel, [len(t) for t in tables], causal),
        "forward",
        [q, *[x for t in tables for x in t]],
        weight_shapes(tables) + [STAT, STAT, WIDE],
        score_shapes(tables) + turned_shapes(tables),
        cost(tables, 2, share),
    )
    return out[:n], out[n:]


def forward_first(*sources):
    tables = [sources[1:3]]
    out = call(
        first_kernel,
        "forward_first",
        sources,
        weight_shapes(tables)
        + [STAT, STAT, WIDE]
        + [pltpu.VMEM(x.shape, x.dtype) for x in sources],
        score_shapes(tables) + turned_shapes(tables) + [pltpu.SemaphoreType.DMA((3,))],
        cost(tables, 2),
        [pl.BlockSpec(memory_space=pl.ANY)] * 3,
        pltpu.CompilerParams(vmem_limit_bytes=FIRST_VMEM * 1024 * 1024),
    )
    return out[:1], out[1:4], out[4:]


def forward_merge(length, q, dout, tables, old):
    n = len(tables)
    e = len(old)
    operands = [length, q, dout, *[t for (t,) in tables], *[x for part in old for x in part]]
    out = call(
        functools.partial(merge_kernel, n, e),
        "forward_merge",
        operands,
        weight_shapes(tables) + [STAT] * (e + 2) + [pltpu.VMEM((HEADS * HD, SLOTS), BF16)],
        score_shapes(tables) + turned_shapes(tables),
        cost(tables, 2),
        [pl.BlockSpec(memory_space=pltpu.SMEM)] + [IN_VMEM] * (len(operands) - 1),
    )
    return out[:n], out[n : n + e + 1], out[n + e + 1], out[n + e + 2]


def backward(q, dout, delta, alphas, tables, weights, kind, dq, last):
    flat = [x for t in tables for x in t]
    kinds = [kind if len(t) == 1 else BF16 for t in tables for _ in t]
    out = call(
        functools.partial(bwd_kernel, [len(t) for t in tables], dq is None, last),
        "backward",
        [q, dout, delta, *alphas, *flat, *weights, *([] if dq is None else [dq])],
        [jax.ShapeDtypeStruct(t.shape, k) for t, k in zip(flat, kinds)]
        + [jax.ShapeDtypeStruct((SLOTS, HEADS * HD), BF16) if last else WIDE],
        turned_shapes(tables)
        + weight_shapes(tables)
        + [pltpu.VMEM((HD, HEADS * SLOTS), BF16) for _ in tables]
        + [pltpu.VMEM((HEADS * SLOTS, HD), BF16)],
        cost(tables, 4),
    )
    return out[:-1], out[-1]


def group_flip(dz, dx):
    return [(z * 4 + x, (z ^ dz) * 4 + (x ^ dx)) for z in range(4) for x in range(4)]


def tensor_flip(bits):
    return [(t, t ^ bits) for t in range(4)]


def per_device(
    queries, comp_keys, comp_values, prompt_keys, prompt_values, out_weight, cotangent, lengths
):
    q = queries[0, 0]
    cot = cotangent[0, 0]

    def over_z(a, s):
        return lax.ppermute(a, "group", group_flip(s, 0))

    def over_x(a, s):
        return lax.ppermute(a, "group", group_flip(0, s))

    def to_core(a):
        return lax.ppermute(a, "tensor", tensor_flip(1))

    def to_chip(a):
        return lax.ppermute(a, "tensor", tensor_flip(2))

    own = jnp.concatenate([prompt_keys[0], prompt_values[0]], axis=1)
    own, comp_k = lax.optimization_barrier((own, comp_keys[0, 0]))
    wc, partc, (q, comp_k, comp_v) = forward_first(q, comp_k, comp_values[0, 0])
    comp = (comp_k, comp_v)
    (topc, totalc, accc), cot_late = lax.optimization_barrier((partc, cot))
    partc = (topc, totalc, accc)
    chunk0 = jnp.concatenate([own] + [over_z(own, s) for s in (1, 3, 2)], axis=0)
    chunk1, chunk3 = over_x(chunk0, 1), over_x(chunk0, 3)
    chunk2 = over_x(chunk1, 3)

    me = lax.axis_index("tensor")

    def columns(bits):
        return lax.dynamic_slice_in_dim(out_weight, (me ^ bits) * 1024, 1024, 1)

    cot_core = to_core(cot)
    cot_chip = to_chip(cot_late)
    cot_diag = to_core(cot_chip)
    w0, part0 = forward(q, [(chunk0,)], (False,), 0.02)
    part0, cot = lax.optimization_barrier((part0, cot))
    half = dot_nt(columns(0), cot) + dot_nt(columns(1), cot_core)
    half, chunk1, chunk3 = lax.optimization_barrier((half, chunk1, chunk3))
    w13, part13 = forward(q, [(chunk1,), (chunk3,)], (False, False))
    dout = (half + dot_nt(columns(2), cot_chip) + dot_nt(columns(3), cot_diag)).astype(BF16)
    w2, (alphac, alpha0, alpha13, alpha2), delta, mixed = forward_merge(
        lengths, q, dout, [(chunk2,)], [partc, part0, part13]
    )
    (g2,), dq = backward(q, dout, delta, [alpha2], [(chunk2,)], w2, BF16, None, False)

    def partial_out(bits):
        block = lax.dot_general(
            mixed, columns(bits), (((0,), (0,)), ((), ())), preferred_element_type=F32
        )
        return block.astype(BF16)

    other = to_core(jnp.concatenate([partial_out(1), partial_out(3)], axis=0))
    other, dq = lax.optimization_barrier((other, dq))
    pair_mine = partial_out(0).astype(F32) + other[:SLOTS].astype(F32)
    pair_far = partial_out(2).astype(F32) + other[SLOTS:].astype(F32)
    pair_far, alpha13 = lax.optimization_barrier((pair_far.astype(BF16), alpha13))
    far = to_chip(pair_far)
    (g1, g3), dq = backward(
        q, dout, delta, [alpha13, alpha13], [(chunk1,), (chunk3,)], w13, BF16, dq, False
    )
    (g0, gck, gcv), dq = backward(
        q, dout, delta, [alpha0, alphac], [(chunk0,), comp], [*w0, *wc], F32, dq, True
    )

    back2, far = lax.optimization_barrier((over_x(g2, 2), far))
    back1, back3 = over_x(g1, 1), over_x(g3, 3)
    rows = g0 + back2.astype(F32) + back1.astype(F32) + back3.astype(F32)
    n = own.shape[0]
    sent = rows.astype(BF16)
    shares = [rows[:n]]
    for i, s in enumerate((1, 3, 2)):
        shares.append(over_z(sent[(i + 1) * n : (i + 2) * n], s).astype(F32))
    key_grad = sum(x[:, :HD] for x in shares).astype(BF16)
    value_grad = sum(x[:, HD:] for x in shares).astype(BF16)
    output = (pair_mine + far.astype(F32)).astype(BF16)
    return (
        output[None, None],
        dq[None, None],
        gck[None, None],
        gcv[None, None],
        key_grad[None],
        value_grad[None],
    )


def solution(mesh):
    wide = P("dp", "group", None, "tensor")
    rows = P("dp", "group", "tensor")
    return jax.shard_map(
        per_device,
        mesh=mesh,
        in_specs=(wide, wide, wide, rows, rows, P("tensor", None), wide, P("dp", "group")),
        out_specs=(wide, wide, wide, wide, rows, rows),
        check_vma=False,
    )
```

```python
import functools

import jax
import jax.numpy as jnp
from jax import lax
from jax.experimental import pallas as pl
from jax.experimental.pallas import tpu as pltpu
from jax.sharding import PartitionSpec as P

HD = 128
HEADS = 8
SLOTS = 256
NEG_FILL = -1e30
LOG2E = 1.4426950408889634
SCALE = HD**-0.5
F32 = jnp.float32
BF16 = jnp.bfloat16
FETCH_VMEM = 56


def dot_nn(a, b):
    return lax.dot_general(a, b, (((1,), (0,)), ((), ())), preferred_element_type=F32)


def dot_nt(a, b):
    return lax.dot_general(a, b, (((1,), (1,)), ((), ())), preferred_element_type=F32)


def span(i):
    return slice(i * HD, (i + 1) * HD)


def wide(i):
    return slice(i * SLOTS, (i + 1) * SLOTS)


def keys(table):
    return table[0][...] if len(table) == 2 else table[0][:, :HD]


def values(table):
    return table[1][...] if len(table) == 2 else table[0][:, HD:]


def regroup(refs, widths):
    refs = iter(refs)
    return [tuple(next(refs) for _ in range(w)) for w in widths]


def attend(q, tables, causal, weights, scores, turned):
    for table, t in zip(tables, turned):
        t[...] = values(table).T
    for i in range(HEADS):
        for table, masked, score in zip(tables, causal, scores):
            s = dot_nt(keys(table), q[:, span(i)]) * (SCALE * LOG2E)
            if masked:
                key = lax.broadcasted_iota(jnp.int32, s.shape, 0)
                token = lax.broadcasted_iota(jnp.int32, s.shape, 1)
                s = jnp.where(key <= token, s, NEG_FILL)
            score[i] = s
    stats = []
    for i in range(HEADS):
        top = functools.reduce(
            jnp.maximum, [jnp.max(score[i], axis=0, keepdims=True) for score in scores]
        )
        total = 0.0
        for score, w in zip(scores, weights):
            p = jnp.exp2(score[i] - top)
            total = total + jnp.sum(p, axis=0, keepdims=True)
            w[:, wide(i)] = p.astype(BF16)
        stats.append((top, total))
    return stats


def mix(i, weights, turned):
    return sum(dot_nn(t[...], w[:, wide(i)]) for t, w in zip(turned, weights))


def fwd_kernel(widths, causal, *refs):
    count = len(widths)
    q = refs[0]
    at = 1 + sum(widths)
    tables = regroup(refs[1:at], widths)
    weights = refs[at : at + count]
    top_ref, total_ref, acc_ref = refs[at + count : at + count + 3]
    scores = refs[at + count + 3 : at + 2 * count + 3]
    turned = refs[at + 2 * count + 3 :]
    stats = attend(q, tables, causal, weights, scores, turned)
    for i in range(HEADS):
        top_ref[i], total_ref[i] = stats[i]
        acc_ref[span(i), :] = mix(i, weights, turned)


def fetch_kernel(*refs):
    sources, held, sems = refs[:3], refs[3:6], refs[6]
    copies = [
        pltpu.make_async_copy(source, target, sems.at[i])
        for i, (source, target) in enumerate(zip(sources, held))
    ]
    for copy in copies:
        copy.start()
    for copy in copies:
        copy.wait()


def merge_kernel(count, earlier, *refs):
    length, q, dout = refs[:3]
    tables = [(t,) for t in refs[3 : 3 + count]]
    at = 3 + count
    old = [refs[at + 3 * i : at + 3 * i + 3] for i in range(earlier)]
    at += 3 * earlier
    weights = refs[at : at + count]
    at += count
    alphas = refs[at : at + earlier + 1]
    delta_ref, mixed_ref = refs[at + earlier + 1 : at + earlier + 3]
    at += earlier + 3
    scores = refs[at : at + count]
    turned = refs[at + count :]
    stats = attend(q, tables, (False,) * count, weights, scores, turned)
    for i in range(HEADS):
        parts = [(t[i], l[i], a[span(i), :]) for t, l, a in old]
        parts.append((*stats[i], mix(i, weights, turned)))
        top = functools.reduce(jnp.maximum, [t for t, _, _ in parts])
        factors = [jnp.exp2(t - top) for t, _, _ in parts]
        total = sum(f * l for f, (_, l, _) in zip(factors, parts))
        live = lax.broadcasted_iota(jnp.int32, top.shape, 1) < length[0, 0]
        inverse = jnp.where(live, 1.0 / total, 0.0)
        mixed = 0.0
        for f, (_, _, acc), alpha in zip(factors, parts, alphas):
            alpha[i] = f * inverse
            mixed = mixed + (f * inverse) * acc
        delta_ref[i] = jnp.sum(mixed * dout[span(i), :].astype(F32), axis=0, keepdims=True)
        mixed_ref[span(i), :] = mixed.astype(BF16)


def bwd_kernel(widths, first, last, *refs):
    count = len(widths)
    q, dout, delta = refs[:3]
    alphas = refs[3 : 3 + count]
    at = 3 + count
    tables = regroup(refs[at : at + sum(widths)], widths)
    at += sum(widths)
    weights = refs[at : at + count]
    at += count
    if not first:
        dq_in = refs[at]
        at += 1
    grads = regroup(refs[at : at + sum(widths)], widths)
    at += sum(widths)
    dq_ref = refs[at]
    turned = refs[at + 1 : at + count + 1]
    slopes = refs[at + count + 1 : at + 2 * count + 1]
    scaled = refs[at + 2 * count + 1 : at + 3 * count + 1]
    (rows,) = refs[at + 3 * count + 1 :]
    for table, t in zip(tables, turned):
        t[...] = keys(table).T
    for i in range(HEADS):
        rows[wide(i), :] = q[:, span(i)]
        for table, alpha, w, ds, da in zip(tables, alphas, weights, slopes, scaled):
            da[:, wide(i)] = (dout[span(i), :].astype(F32) * alpha[i]).astype(BF16)
            dp = dot_nn(values(table), da[:, wide(i)])
            p = w[:, wide(i)].astype(F32)
            ds[:, wide(i)] = (p * (dp - delta[i] * alpha[i])).astype(BF16)
    for w, ds, da, g in zip(weights, slopes, scaled, grads):
        low, high = dot_nn(ds[...], rows[...]) * SCALE, dot_nt(w[...], da[...])
        if len(g) == 2:
            g[0][...], g[1][...] = low.astype(g[0].dtype), high.astype(g[1].dtype)
        else:
            g[0][:, :HD], g[0][:, HD:] = low.astype(g[0].dtype), high.astype(g[0].dtype)
    for i in range(HEADS):
        dq = sum(dot_nn(kt[...], ds[:, wide(i)]) for kt, ds in zip(turned, slopes))
        if not first:
            dq = dq + dq_in[span(i), :]
        if last:
            dq_ref[:, span(i)] = (dq * SCALE).T.astype(dq_ref.dtype)
        else:
            dq_ref[span(i), :] = dq


IN_VMEM = pl.BlockSpec(memory_space=pltpu.VMEM)
STAT = pltpu.VMEM((HEADS, 1, SLOTS), F32)
WIDE = pltpu.VMEM((HEADS * HD, SLOTS), F32)
PARAMS = pltpu.CompilerParams(vmem_limit_bytes=20 * 1024 * 1024)


def call(kernel, name, operands, shapes, scratch, cost, specs=None, params=PARAMS):
    return pl.pallas_call(
        kernel,
        in_specs=specs or [IN_VMEM] * len(operands),
        out_specs=[IN_VMEM] * len(shapes),
        out_shape=shapes,
        scratch_shapes=scratch,
        cost_estimate=cost,
        compiler_params=params,
        name=name,
    )(*operands)


def weight_shapes(tables):
    return [pltpu.VMEM((t.shape[0], HEADS * SLOTS), BF16) for (t, *_) in tables]


def score_shapes(tables):
    return [pltpu.VMEM((HEADS, t.shape[0], SLOTS), F32) for (t, *_) in tables]


def turned_shapes(tables):
    return [pltpu.VMEM((HD, t.shape[0]), BF16) for (t, *_) in tables]


def cost(tables, dots, share=16):
    rows = sum(t[0].shape[0] for t in tables)
    area = rows * SLOTS * HEADS
    return pl.CostEstimate(
        flops=int(dots * area * HD / share), bytes_accessed=area // 16, transcendentals=0
    )


def forward(q, tables, causal, share=16):
    n = len(tables)
    out = call(
        functools.partial(fwd_kernel, [len(t) for t in tables], causal),
        "forward",
        [q, *[x for t in tables for x in t]],
        weight_shapes(tables) + [STAT, STAT, WIDE],
        score_shapes(tables) + turned_shapes(tables),
        cost(tables, 2, share),
    )
    return out[:n], out[n:]


def fetch(*sources):
    return call(
        fetch_kernel,
        "fetch",
        sources,
        [pltpu.VMEM(x.shape, x.dtype) for x in sources],
        [pltpu.SemaphoreType.DMA((3,))],
        pl.CostEstimate(flops=10**6, bytes_accessed=10**5, transcendentals=0),
        [pl.BlockSpec(memory_space=pl.ANY)] * 3,
        pltpu.CompilerParams(vmem_limit_bytes=FETCH_VMEM * 1024 * 1024),
    )


def forward_merge(length, q, dout, tables, old):
    n = len(tables)
    e = len(old)
    operands = [length, q, dout, *[t for (t,) in tables], *[x for part in old for x in part]]
    out = call(
        functools.partial(merge_kernel, n, e),
        "forward_merge",
        operands,
        weight_shapes(tables) + [STAT] * (e + 2) + [pltpu.VMEM((HEADS * HD, SLOTS), BF16)],
        score_shapes(tables) + turned_shapes(tables),
        cost(tables, 2),
        [pl.BlockSpec(memory_space=pltpu.SMEM)] + [IN_VMEM] * (len(operands) - 1),
    )
    return out[:n], out[n : n + e + 1], out[n + e + 1], out[n + e + 2]


def backward(q, dout, delta, alphas, tables, weights, kind, dq, last):
    flat = [x for t in tables for x in t]
    kinds = [kind if len(t) == 1 else BF16 for t in tables for _ in t]
    out = call(
        functools.partial(bwd_kernel, [len(t) for t in tables], dq is None, last),
        "backward",
        [q, dout, delta, *alphas, *flat, *weights, *([] if dq is None else [dq])],
        [jax.ShapeDtypeStruct(t.shape, k) for t, k in zip(flat, kinds)]
        + [jax.ShapeDtypeStruct((SLOTS, HEADS * HD), BF16) if last else WIDE],
        turned_shapes(tables)
        + weight_shapes(tables)
        + [pltpu.VMEM((HD, HEADS * SLOTS), BF16) for _ in tables]
        + [pltpu.VMEM((HEADS * SLOTS, HD), BF16)],
        cost(tables, 4),
    )
    return out[:-1], out[-1]


def group_flip(dz, dx):
    return [(z * 4 + x, (z ^ dz) * 4 + (x ^ dx)) for z in range(4) for x in range(4)]


def tensor_flip(bits):
    return [(t, t ^ bits) for t in range(4)]


def per_device(
    queries, comp_keys, comp_values, prompt_keys, prompt_values, out_weight, cotangent, lengths
):
    q = queries[0, 0]
    cot = cotangent[0, 0]

    def over_z(a, s):
        return lax.ppermute(a, "group", group_flip(s, 0))

    def over_x(a, s):
        return lax.ppermute(a, "group", group_flip(0, s))

    def to_core(a):
        return lax.ppermute(a, "tensor", tensor_flip(1))

    def to_chip(a):
        return lax.ppermute(a, "tensor", tensor_flip(2))

    own = jnp.concatenate([prompt_keys[0], prompt_values[0]], axis=1)
    own, comp_k = lax.optimization_barrier((own, comp_keys[0, 0]))
    q, comp_k, comp_v = fetch(q, comp_k, comp_values[0, 0])
    comp = (comp_k, comp_v)
    q, cot_late = lax.optimization_barrier((q, cot))
    chunk0 = jnp.concatenate([own] + [over_z(own, s) for s in (1, 3, 2)], axis=0)
    chunk1, chunk3 = over_x(chunk0, 1), over_x(chunk0, 3)
    chunk2 = over_x(chunk1, 3)

    me = lax.axis_index("tensor")

    def columns(bits):
        return lax.dynamic_slice_in_dim(out_weight, (me ^ bits) * 1024, 1024, 1)

    cot_core = to_core(cot)
    cot_chip = to_chip(cot_late)
    cot_diag = to_core(cot_chip)
    w0, part0 = forward(q, [(chunk0,), comp], (False, True), 0.02)
    part0, cot = lax.optimization_barrier((part0, cot))
    half = dot_nt(columns(0), cot) + dot_nt(columns(1), cot_core)
    half, chunk1, chunk3 = lax.optimization_barrier((half, chunk1, chunk3))
    w13, part13 = forward(q, [(chunk1,), (chunk3,)], (False, False))
    dout = (half + dot_nt(columns(2), cot_chip) + dot_nt(columns(3), cot_diag)).astype(BF16)
    w2, (alpha0, alpha13, alpha2), delta, mixed = forward_merge(
        lengths, q, dout, [(chunk2,)], [part0, part13]
    )
    (g2,), dq = backward(q, dout, delta, [alpha2], [(chunk2,)], w2, BF16, None, False)

    def partial_out(bits):
        block = lax.dot_general(
            mixed, columns(bits), (((0,), (0,)), ((), ())), preferred_element_type=F32
        )
        return block.astype(BF16)

    other = to_core(jnp.concatenate([partial_out(1), partial_out(3)], axis=0))
    other, dq = lax.optimization_barrier((other, dq))
    pair_mine = partial_out(0).astype(F32) + other[:SLOTS].astype(F32)
    pair_far = partial_out(2).astype(F32) + other[SLOTS:].astype(F32)
    pair_far, alpha13 = lax.optimization_barrier((pair_far.astype(BF16), alpha13))
    far = to_chip(pair_far)
    (g1, g3), dq = backward(
        q, dout, delta, [alpha13, alpha13], [(chunk1,), (chunk3,)], w13, BF16, dq, False
    )
    (g0, gck, gcv), dq = backward(
        q, dout, delta, [alpha0, alpha0], [(chunk0,), comp], w0, F32, dq, True
    )

    back2, far = lax.optimization_barrier((over_x(g2, 2), far))
    back1, back3 = over_x(g1, 1), over_x(g3, 3)
    rows = g0 + back2.astype(F32) + back1.astype(F32) + back3.astype(F32)
    n = own.shape[0]
    sent = rows.astype(BF16)
    shares = [rows[:n]]
    for i, s in enumerate((1, 3, 2)):
        shares.append(over_z(sent[(i + 1) * n : (i + 2) * n], s).astype(F32))
    key_grad = sum(x[:, :HD] for x in shares).astype(BF16)
    value_grad = sum(x[:, HD:] for x in shares).astype(BF16)
    output = (pair_mine + far.astype(F32)).astype(BF16)
    return (
        output[None, None],
        dq[None, None],
        gck[None, None],
        gcv[None, None],
        key_grad[None],
        value_grad[None],
    )


def solution(mesh):
    wide = P("dp", "group", None, "tensor")
    rows = P("dp", "group", "tensor")
    return jax.shard_map(
        per_device,
        mesh=mesh,
        in_specs=(wide, wide, wide, rows, rows, P("tensor", None), wide, P("dp", "group")),
        out_specs=(wide, wide, wide, wide, rows, rows),
        check_vma=False,
    )
```

```python
import functools

import jax
import jax.numpy as jnp
from jax import lax
from jax.experimental import pallas as pl
from jax.experimental.pallas import tpu as pltpu
from jax.sharding import PartitionSpec as P

HD = 128
HEADS = 8
SLOTS = 256
NEG_FILL = -1e30
LOG2E = 1.4426950408889634
SCALE = HD**-0.5
F32 = jnp.float32
BF16 = jnp.bfloat16
FETCH_VMEM = 56


def dot_nn(a, b):
    return lax.dot_general(a, b, (((1,), (0,)), ((), ())), preferred_element_type=F32)


def dot_nt(a, b):
    return lax.dot_general(a, b, (((1,), (1,)), ((), ())), preferred_element_type=F32)


def span(i):
    return slice(i * HD, (i + 1) * HD)


def wide(i):
    return slice(i * SLOTS, (i + 1) * SLOTS)


def keys(table):
    return table[0][...] if len(table) == 2 else table[0][:, :HD]


def values(table):
    return table[1][...] if len(table) == 2 else table[0][:, HD:]


def regroup(refs, widths):
    refs = iter(refs)
    return [tuple(next(refs) for _ in range(w)) for w in widths]


def attend(q, tables, causal, weights, scores, turned):
    for table, t in zip(tables, turned):
        t[...] = values(table).T
    for i in range(HEADS):
        for table, masked, score in zip(tables, causal, scores):
            s = dot_nt(keys(table), q[:, span(i)]) * (SCALE * LOG2E)
            if masked:
                key = lax.broadcasted_iota(jnp.int32, s.shape, 0)
                token = lax.broadcasted_iota(jnp.int32, s.shape, 1)
                s = jnp.where(key <= token, s, NEG_FILL)
            score[i] = s
    stats = []
    for i in range(HEADS):
        top = functools.reduce(
            jnp.maximum, [jnp.max(score[i], axis=0, keepdims=True) for score in scores]
        )
        total = 0.0
        for score, w in zip(scores, weights):
            p = jnp.exp2(score[i] - top)
            total = total + jnp.sum(p, axis=0, keepdims=True)
            w[:, wide(i)] = p.astype(BF16)
        stats.append((top, total))
    return stats


def mix(i, weights, turned):
    return sum(dot_nn(t[...], w[:, wide(i)]) for t, w in zip(turned, weights))


def fwd_kernel(widths, causal, *refs):
    count = len(widths)
    q = refs[0]
    at = 1 + sum(widths)
    tables = regroup(refs[1:at], widths)
    weights = refs[at : at + count]
    top_ref, total_ref, acc_ref = refs[at + count : at + count + 3]
    scores = refs[at + count + 3 : at + 2 * count + 3]
    turned = refs[at + 2 * count + 3 :]
    stats = attend(q, tables, causal, weights, scores, turned)
    for i in range(HEADS):
        top_ref[i], total_ref[i] = stats[i]
        acc_ref[span(i), :] = mix(i, weights, turned)


def fetch_kernel(*refs):
    sources, held, sems = refs[:3], refs[3:6], refs[6]
    copies = [
        pltpu.make_async_copy(source, target, sems.at[i])
        for i, (source, target) in enumerate(zip(sources, held))
    ]
    for copy in copies:
        copy.start()
    for copy in copies:
        copy.wait()


def merge_kernel(count, earlier, *refs):
    length, q, dout = refs[:3]
    tables = [(t,) for t in refs[3 : 3 + count]]
    at = 3 + count
    old = [refs[at + 3 * i : at + 3 * i + 3] for i in range(earlier)]
    at += 3 * earlier
    weights = refs[at : at + count]
    at += count
    alphas = refs[at : at + earlier + 1]
    delta_ref, mixed_ref = refs[at + earlier + 1 : at + earlier + 3]
    at += earlier + 3
    scores = refs[at : at + count]
    turned = refs[at + count :]
    stats = attend(q, tables, (False,) * count, weights, scores, turned)
    for i in range(HEADS):
        parts = [(t[i], l[i], a[span(i), :]) for t, l, a in old]
        parts.append((*stats[i], mix(i, weights, turned)))
        top = functools.reduce(jnp.maximum, [t for t, _, _ in parts])
        factors = [jnp.exp2(t - top) for t, _, _ in parts]
        total = sum(f * l for f, (_, l, _) in zip(factors, parts))
        live = lax.broadcasted_iota(jnp.int32, top.shape, 1) < length[0, 0]
        inverse = jnp.where(live, 1.0 / total, 0.0)
        mixed = 0.0
        for f, (_, _, acc), alpha in zip(factors, parts, alphas):
            alpha[i] = f * inverse
            mixed = mixed + (f * inverse) * acc
        delta_ref[i] = jnp.sum(mixed * dout[span(i), :].astype(F32), axis=0, keepdims=True)
        mixed_ref[span(i), :] = mixed.astype(BF16)


def bwd_kernel(widths, first, last, joined, *refs):
    count = len(widths)
    q, dout, delta = refs[:3]
    alphas = refs[3 : 3 + count]
    at = 3 + count
    tables = regroup(refs[at : at + sum(widths)], widths)
    at += sum(widths)
    weights = refs[at : at + count]
    at += count
    if not first:
        dq_in = refs[at]
        at += 1
    if joined:
        n = tables[0][0].shape[0]
        grads = [(refs[at].at[i * n : (i + 1) * n],) for i in range(count)]
        at += 1
    else:
        grads = regroup(refs[at : at + sum(widths)], widths)
        at += sum(widths)
    dq_ref = refs[at]
    turned = refs[at + 1 : at + count + 1]
    slopes = refs[at + count + 1 : at + 2 * count + 1]
    scaled = refs[at + 2 * count + 1 : at + 3 * count + 1]
    (rows,) = refs[at + 3 * count + 1 :]
    for table, t in zip(tables, turned):
        t[...] = keys(table).T
    for i in range(HEADS):
        rows[wide(i), :] = q[:, span(i)]
        for table, alpha, w, ds, da in zip(tables, alphas, weights, slopes, scaled):
            da[:, wide(i)] = (dout[span(i), :].astype(F32) * alpha[i]).astype(BF16)
            dp = dot_nn(values(table), da[:, wide(i)])
            p = w[:, wide(i)].astype(F32)
            ds[:, wide(i)] = (p * (dp - delta[i] * alpha[i])).astype(BF16)
    for w, ds, da, g in zip(weights, slopes, scaled, grads):
        low, high = dot_nn(ds[...], rows[...]) * SCALE, dot_nt(w[...], da[...])
        if len(g) == 2:
            g[0][...], g[1][...] = low.astype(g[0].dtype), high.astype(g[1].dtype)
        else:
            g[0][:, :HD], g[0][:, HD:] = low.astype(g[0].dtype), high.astype(g[0].dtype)
    for i in range(HEADS):
        dq = sum(dot_nn(kt[...], ds[:, wide(i)]) for kt, ds in zip(turned, slopes))
        if not first:
            dq = dq + dq_in[span(i), :]
        if last:
            dq_ref[:, span(i)] = (dq * SCALE).T.astype(dq_ref.dtype)
        else:
            dq_ref[span(i), :] = dq


IN_VMEM = pl.BlockSpec(memory_space=pltpu.VMEM)
STAT = pltpu.VMEM((HEADS, 1, SLOTS), F32)
WIDE = pltpu.VMEM((HEADS * HD, SLOTS), F32)
PARAMS = pltpu.CompilerParams(vmem_limit_bytes=20 * 1024 * 1024)


def call(kernel, name, operands, shapes, scratch, cost, specs=None, params=PARAMS):
    return pl.pallas_call(
        kernel,
        in_specs=specs or [IN_VMEM] * len(operands),
        out_specs=[IN_VMEM] * len(shapes),
        out_shape=shapes,
        scratch_shapes=scratch,
        cost_estimate=cost,
        compiler_params=params,
        name=name,
    )(*operands)


def weight_shapes(tables):
    return [pltpu.VMEM((t.shape[0], HEADS * SLOTS), BF16) for (t, *_) in tables]


def score_shapes(tables):
    return [pltpu.VMEM((HEADS, t.shape[0], SLOTS), F32) for (t, *_) in tables]


def turned_shapes(tables):
    return [pltpu.VMEM((HD, t.shape[0]), BF16) for (t, *_) in tables]


def cost(tables, dots, share=16):
    rows = sum(t[0].shape[0] for t in tables)
    area = rows * SLOTS * HEADS
    return pl.CostEstimate(
        flops=int(dots * area * HD / share), bytes_accessed=area // 16, transcendentals=0
    )


def forward(q, tables, causal, share=16):
    n = len(tables)
    out = call(
        functools.partial(fwd_kernel, [len(t) for t in tables], causal),
        "forward",
        [q, *[x for t in tables for x in t]],
        weight_shapes(tables) + [STAT, STAT, WIDE],
        score_shapes(tables) + turned_shapes(tables),
        cost(tables, 2, share),
    )
    return out[:n], out[n:]


def fetch(*sources):
    return call(
        fetch_kernel,
        "fetch",
        sources,
        [pltpu.VMEM(x.shape, x.dtype) for x in sources],
        [pltpu.SemaphoreType.DMA((3,))],
        pl.CostEstimate(flops=10**6, bytes_accessed=10**5, transcendentals=0),
        [pl.BlockSpec(memory_space=pl.ANY)] * 3,
        pltpu.CompilerParams(vmem_limit_bytes=FETCH_VMEM * 1024 * 1024),
    )


def forward_merge(length, q, dout, tables, old):
    n = len(tables)
    e = len(old)
    operands = [length, q, dout, *[t for (t,) in tables], *[x for part in old for x in part]]
    out = call(
        functools.partial(merge_kernel, n, e),
        "forward_merge",
        operands,
        weight_shapes(tables) + [STAT] * (e + 2) + [pltpu.VMEM((HEADS * HD, SLOTS), BF16)],
        score_shapes(tables) + turned_shapes(tables),
        cost(tables, 2),
        [pl.BlockSpec(memory_space=pltpu.SMEM)] + [IN_VMEM] * (len(operands) - 1),
    )
    return out[:n], out[n : n + e + 1], out[n + e + 1], out[n + e + 2]


def backward(q, dout, delta, alphas, tables, weights, kind, dq, last, joined=False):
    flat = [x for t in tables for x in t]
    shapes = [t.shape for t in flat]
    if joined:
        shapes = [(sum(t.shape[0] for t in flat), flat[0].shape[1])]
    kinds = [kind if len(t) == 1 else BF16 for t in tables for _ in t]
    out = call(
        functools.partial(bwd_kernel, [len(t) for t in tables], dq is None, last, joined),
        "backward",
        [q, dout, delta, *alphas, *flat, *weights, *([] if dq is None else [dq])],
        [jax.ShapeDtypeStruct(shape, k) for shape, k in zip(shapes, kinds)]
        + [jax.ShapeDtypeStruct((SLOTS, HEADS * HD), BF16) if last else WIDE],
        turned_shapes(tables)
        + weight_shapes(tables)
        + [pltpu.VMEM((HD, HEADS * SLOTS), BF16) for _ in tables]
        + [pltpu.VMEM((HEADS * SLOTS, HD), BF16)],
        cost(tables, 4),
    )
    return out[:-1], out[-1]


def group_flip(dz, dx):
    return [(z * 4 + x, (z ^ dz) * 4 + (x ^ dx)) for z in range(4) for x in range(4)]


def tensor_flip(bits):
    return [(t, t ^ bits) for t in range(4)]


def per_device(
    queries, comp_keys, comp_values, prompt_keys, prompt_values, out_weight, cotangent, lengths
):
    q = queries[0, 0]
    cot = cotangent[0, 0]

    def over_z(a, s):
        return lax.ppermute(a, "group", group_flip(s, 0))

    def over_x(a, s):
        return lax.ppermute(a, "group", group_flip(0, s))

    def to_core(a):
        return lax.ppermute(a, "tensor", tensor_flip(1))

    def to_chip(a):
        return lax.ppermute(a, "tensor", tensor_flip(2))

    own = jnp.concatenate([prompt_keys[0], prompt_values[0]], axis=1)
    own, comp_k = lax.optimization_barrier((own, comp_keys[0, 0]))
    q, comp_k, comp_v = fetch(q, comp_k, comp_values[0, 0])
    comp = (comp_k, comp_v)
    q, cot_late = lax.optimization_barrier((q, cot))
    chunk0 = jnp.concatenate([own] + [over_z(own, s) for s in (1, 3, 2)], axis=0)
    chunk1, chunk3 = over_x(chunk0, 1), over_x(chunk0, 3)
    middle = chunk0.shape[0] // 2
    halves = [(over_x(chunk1[:middle], 3),), (over_x(chunk3[middle:], 1),)]

    me = lax.axis_index("tensor")

    def columns(bits):
        return lax.dynamic_slice_in_dim(out_weight, (me ^ bits) * 1024, 1024, 1)

    cot_core = to_core(cot)
    cot_chip = to_chip(cot_late)
    cot_diag = to_core(cot_chip)
    w0, part0 = forward(q, [(chunk0,), comp], (False, True), 0.03)
    part0, cot = lax.optimization_barrier((part0, cot))
    half = dot_nt(columns(0), cot) + dot_nt(columns(1), cot_core)
    half, chunk1, chunk3 = lax.optimization_barrier((half, chunk1, chunk3))
    w13, part13 = forward(q, [(chunk1,), (chunk3,)], (False, False))
    dout = (half + dot_nt(columns(2), cot_chip) + dot_nt(columns(3), cot_diag)).astype(BF16)
    w2, (alpha0, alpha13, alpha2), delta, mixed = forward_merge(
        lengths, q, dout, halves, [part0, part13]
    )
    (g2,), dq = backward(q, dout, delta, [alpha2, alpha2], halves, w2, BF16, None, False, True)

    def partial_out(bits):
        block = lax.dot_general(
            mixed, columns(bits), (((0,), (0,)), ((), ())), preferred_element_type=F32
        )
        return block.astype(BF16)

    other = to_core(jnp.concatenate([partial_out(1), partial_out(3)], axis=0))
    other, dq = lax.optimization_barrier((other, dq))
    pair_mine = partial_out(0).astype(F32) + other[:SLOTS].astype(F32)
    pair_far = partial_out(2).astype(F32) + other[SLOTS:].astype(F32)
    pair_far, alpha13 = lax.optimization_barrier((pair_far.astype(BF16), alpha13))
    far = to_chip(pair_far)
    (g1, g3), dq = backward(
        q, dout, delta, [alpha13, alpha13], [(chunk1,), (chunk3,)], w13, BF16, dq, False
    )
    (g0, gck, gcv), dq = backward(
        q, dout, delta, [alpha0, alpha0], [(chunk0,), comp], w0, F32, dq, True
    )

    back2, far = lax.optimization_barrier((over_x(g2, 2), far))
    back1, back3 = over_x(g1, 1), over_x(g3, 3)
    rows = g0 + back2.astype(F32) + back1.astype(F32) + back3.astype(F32)
    n = own.shape[0]
    sent = rows.astype(BF16)
    shares = [rows[:n]]
    for i, s in enumerate((1, 3, 2)):
        shares.append(over_z(sent[(i + 1) * n : (i + 2) * n], s).astype(F32))
    key_grad = sum(x[:, :HD] for x in shares).astype(BF16)
    value_grad = sum(x[:, HD:] for x in shares).astype(BF16)
    output = (pair_mine + far.astype(F32)).astype(BF16)
    return (
        output[None, None],
        dq[None, None],
        gck[None, None],
        gcv[None, None],
        key_grad[None],
        value_grad[None],
    )


def solution(mesh):
    wide = P("dp", "group", None, "tensor")
    rows = P("dp", "group", "tensor")
    return jax.shard_map(
        per_device,
        mesh=mesh,
        in_specs=(wide, wide, wide, rows, rows, P("tensor", None), wide, P("dp", "group")),
        out_specs=(wide, wide, wide, wide, rows, rows),
        check_vma=False,
    )
```

```python
import functools

import jax
import jax.numpy as jnp
from jax import lax
from jax.experimental import pallas as pl
from jax.experimental.pallas import tpu as pltpu
from jax.sharding import PartitionSpec as P

HD = 128
HEADS = 8
SLOTS = 256
NEG_FILL = -1e30
LOG2E = 1.4426950408889634
SCALE = HD**-0.5
F32 = jnp.float32
BF16 = jnp.bfloat16
FETCH_VMEM = 56


def dot_nn(a, b):
    return lax.dot_general(a, b, (((1,), (0,)), ((), ())), preferred_element_type=F32)


def dot_nt(a, b):
    return lax.dot_general(a, b, (((1,), (1,)), ((), ())), preferred_element_type=F32)


def span(i):
    return slice(i * HD, (i + 1) * HD)


def wide(i):
    return slice(i * SLOTS, (i + 1) * SLOTS)


def keys(table):
    return table[0][...] if len(table) == 2 else table[0][:, :HD]


def values(table):
    return table[1][...] if len(table) == 2 else table[0][:, HD:]


def regroup(refs, widths):
    refs = iter(refs)
    return [tuple(next(refs) for _ in range(w)) for w in widths]


def attend(q, tables, causal, weights, scores, turned):
    for table, t in zip(tables, turned):
        t[...] = values(table).T
    for i in range(HEADS):
        for table, masked, score in zip(tables, causal, scores):
            s = dot_nt(keys(table), q[:, span(i)]) * (SCALE * LOG2E)
            if masked:
                key = lax.broadcasted_iota(jnp.int32, s.shape, 0)
                token = lax.broadcasted_iota(jnp.int32, s.shape, 1)
                s = jnp.where(key <= token, s, NEG_FILL)
            score[i] = s
    stats = []
    for i in range(HEADS):
        top = functools.reduce(
            jnp.maximum, [jnp.max(score[i], axis=0, keepdims=True) for score in scores]
        )
        total = 0.0
        for score, w in zip(scores, weights):
            p = jnp.exp2(score[i] - top)
            total = total + jnp.sum(p, axis=0, keepdims=True)
            w[:, wide(i)] = p.astype(BF16)
        stats.append((top, total))
    return stats


def mix(i, weights, turned):
    return sum(dot_nn(t[...], w[:, wide(i)]) for t, w in zip(turned, weights))


def fwd_kernel(widths, causal, *refs):
    count = len(widths)
    q = refs[0]
    at = 1 + sum(widths)
    tables = regroup(refs[1:at], widths)
    weights = refs[at : at + count]
    top_ref, total_ref, acc_ref = refs[at + count : at + count + 3]
    scores = refs[at + count + 3 : at + 2 * count + 3]
    turned = refs[at + 2 * count + 3 :]
    stats = attend(q, tables, causal, weights, scores, turned)
    for i in range(HEADS):
        top_ref[i], total_ref[i] = stats[i]
        acc_ref[span(i), :] = mix(i, weights, turned)


def fetch_kernel(*refs):
    sources, held, sems = refs[:3], refs[3:6], refs[6]
    copies = [
        pltpu.make_async_copy(source, target, sems.at[i])
        for i, (source, target) in enumerate(zip(sources, held))
    ]
    for copy in copies:
        copy.start()
    for copy in copies:
        copy.wait()


def merge_kernel(count, earlier, *refs):
    length, q, dout = refs[:3]
    tables = [(t,) for t in refs[3 : 3 + count]]
    at = 3 + count
    old = [refs[at + 3 * i : at + 3 * i + 3] for i in range(earlier)]
    at += 3 * earlier
    weights = refs[at : at + count]
    at += count
    alphas = refs[at : at + earlier + 1]
    delta_ref, mixed_ref = refs[at + earlier + 1 : at + earlier + 3]
    at += earlier + 3
    scores = refs[at : at + count]
    turned = refs[at + count :]
    stats = attend(q, tables, (False,) * count, weights, scores, turned)
    for i in range(HEADS):
        parts = [(t[i], l[i], a[span(i), :]) for t, l, a in old]
        parts.append((*stats[i], mix(i, weights, turned)))
        top = functools.reduce(jnp.maximum, [t for t, _, _ in parts])
        factors = [jnp.exp2(t - top) for t, _, _ in parts]
        total = sum(f * l for f, (_, l, _) in zip(factors, parts))
        live = lax.broadcasted_iota(jnp.int32, top.shape, 1) < length[0, 0]
        inverse = jnp.where(live, 1.0 / total, 0.0)
        mixed = 0.0
        for f, (_, _, acc), alpha in zip(factors, parts, alphas):
            alpha[i] = f * inverse
            mixed = mixed + (f * inverse) * acc
        delta_ref[i] = jnp.sum(mixed * dout[span(i), :].astype(F32), axis=0, keepdims=True)
        mixed_ref[span(i), :] = mixed.astype(BF16)


def bwd_kernel(widths, first, last, *refs):
    count = len(widths)
    q, dout, delta = refs[:3]
    alphas = refs[3 : 3 + count]
    at = 3 + count
    tables = regroup(refs[at : at + sum(widths)], widths)
    at += sum(widths)
    weights = refs[at : at + count]
    at += count
    if not first:
        dq_in = refs[at]
        at += 1
    grads = regroup(refs[at : at + sum(widths)], widths)
    at += sum(widths)
    dq_ref = refs[at]
    turned = refs[at + 1 : at + count + 1]
    slopes = refs[at + count + 1 : at + 2 * count + 1]
    scaled = refs[at + 2 * count + 1 : at + 3 * count + 1]
    (rows,) = refs[at + 3 * count + 1 :]
    for table, t in zip(tables, turned):
        t[...] = keys(table).T
    for i in range(HEADS):
        rows[wide(i), :] = q[:, span(i)]
        for table, alpha, w, ds, da in zip(tables, alphas, weights, slopes, scaled):
            da[:, wide(i)] = (dout[span(i), :].astype(F32) * alpha[i]).astype(BF16)
            dp = dot_nn(values(table), da[:, wide(i)])
            p = w[:, wide(i)].astype(F32)
            ds[:, wide(i)] = (p * (dp - delta[i] * alpha[i])).astype(BF16)
    for w, ds, da, g in zip(weights, slopes, scaled, grads):
        low, high = dot_nn(ds[...], rows[...]) * SCALE, dot_nt(w[...], da[...])
        if len(g) == 2:
            g[0][...], g[1][...] = low.astype(g[0].dtype), high.astype(g[1].dtype)
        else:
            g[0][:, :HD], g[0][:, HD:] = low.astype(g[0].dtype), high.astype(g[0].dtype)
    for i in range(HEADS):
        dq = sum(dot_nn(kt[...], ds[:, wide(i)]) for kt, ds in zip(turned, slopes))
        if not first:
            dq = dq + dq_in[span(i), :]
        if last:
            dq_ref[:, span(i)] = (dq * SCALE).T.astype(dq_ref.dtype)
        else:
            dq_ref[span(i), :] = dq


IN_VMEM = pl.BlockSpec(memory_space=pltpu.VMEM)
STAT = pltpu.VMEM((HEADS, 1, SLOTS), F32)
WIDE = pltpu.VMEM((HEADS * HD, SLOTS), F32)
PARAMS = pltpu.CompilerParams(vmem_limit_bytes=20 * 1024 * 1024)


def call(kernel, name, operands, shapes, scratch, cost, specs=None, params=PARAMS):
    return pl.pallas_call(
        kernel,
        in_specs=specs or [IN_VMEM] * len(operands),
        out_specs=[IN_VMEM] * len(shapes),
        out_shape=shapes,
        scratch_shapes=scratch,
        cost_estimate=cost,
        compiler_params=params,
        name=name,
    )(*operands)


def weight_shapes(tables):
    return [pltpu.VMEM((t.shape[0], HEADS * SLOTS), BF16) for (t, *_) in tables]


def score_shapes(tables):
    return [pltpu.VMEM((HEADS, t.shape[0], SLOTS), F32) for (t, *_) in tables]


def turned_shapes(tables):
    return [pltpu.VMEM((HD, t.shape[0]), BF16) for (t, *_) in tables]


def cost(tables, dots, share=16):
    rows = sum(t[0].shape[0] for t in tables)
    area = rows * SLOTS * HEADS
    return pl.CostEstimate(
        flops=int(dots * area * HD / share), bytes_accessed=area // 16, transcendentals=0
    )


def forward(q, tables, causal, share=16):
    n = len(tables)
    out = call(
        functools.partial(fwd_kernel, [len(t) for t in tables], causal),
        "forward",
        [q, *[x for t in tables for x in t]],
        weight_shapes(tables) + [STAT, STAT, WIDE],
        score_shapes(tables) + turned_shapes(tables),
        cost(tables, 2, share),
    )
    return out[:n], out[n:]


def fetch(*sources):
    return call(
        fetch_kernel,
        "fetch",
        sources,
        [pltpu.VMEM(x.shape, x.dtype) for x in sources],
        [pltpu.SemaphoreType.DMA((3,))],
        pl.CostEstimate(flops=10**6, bytes_accessed=10**5, transcendentals=0),
        [pl.BlockSpec(memory_space=pl.ANY)] * 3,
        pltpu.CompilerParams(vmem_limit_bytes=FETCH_VMEM * 1024 * 1024),
    )


def forward_merge(length, q, dout, tables, old):
    n = len(tables)
    e = len(old)
    operands = [length, q, dout, *[t for (t,) in tables], *[x for part in old for x in part]]
    out = call(
        functools.partial(merge_kernel, n, e),
        "forward_merge",
        operands,
        weight_shapes(tables) + [STAT] * (e + 2) + [pltpu.VMEM((HEADS * HD, SLOTS), BF16)],
        score_shapes(tables) + turned_shapes(tables),
        cost(tables, 2),
        [pl.BlockSpec(memory_space=pltpu.SMEM)] + [IN_VMEM] * (len(operands) - 1),
    )
    return out[:n], out[n : n + e + 1], out[n + e + 1], out[n + e + 2]


def backward(q, dout, delta, alphas, tables, weights, kind, dq, last):
    flat = [x for t in tables for x in t]
    kinds = [kind if len(t) == 1 else BF16 for t in tables for _ in t]
    out = call(
        functools.partial(bwd_kernel, [len(t) for t in tables], dq is None, last),
        "backward",
        [q, dout, delta, *alphas, *flat, *weights, *([] if dq is None else [dq])],
        [jax.ShapeDtypeStruct(t.shape, k) for t, k in zip(flat, kinds)]
        + [jax.ShapeDtypeStruct((SLOTS, HEADS * HD), BF16) if last else WIDE],
        turned_shapes(tables)
        + weight_shapes(tables)
        + [pltpu.VMEM((HD, HEADS * SLOTS), BF16) for _ in tables]
        + [pltpu.VMEM((HEADS * SLOTS, HD), BF16)],
        cost(tables, 4),
    )
    return out[:-1], out[-1]


def group_flip(dz, dx):
    return [(z * 4 + x, (z ^ dz) * 4 + (x ^ dx)) for z in range(4) for x in range(4)]


def tensor_flip(bits):
    return [(t, t ^ bits) for t in range(4)]


def per_device(
    queries, comp_keys, comp_values, prompt_keys, prompt_values, out_weight, cotangent, lengths
):
    q = queries[0, 0]
    cot = cotangent[0, 0]

    def over_z(a, s):
        return lax.ppermute(a, "group", group_flip(s, 0))

    def over_x(a, s):
        return lax.ppermute(a, "group", group_flip(0, s))

    def to_core(a):
        return lax.ppermute(a, "tensor", tensor_flip(1))

    def to_chip(a):
        return lax.ppermute(a, "tensor", tensor_flip(2))

    own = jnp.concatenate([prompt_keys[0], prompt_values[0]], axis=1)
    own, comp_k = lax.optimization_barrier((own, comp_keys[0, 0]))
    q, comp_k, comp_v = fetch(q, comp_k, comp_values[0, 0])
    comp = (comp_k, comp_v)
    q, cot_late = lax.optimization_barrier((q, cot))
    chunk0 = jnp.concatenate([own] + [over_z(own, s) for s in (1, 3, 2)], axis=0)
    chunk1, chunk3 = over_x(chunk0, 1), over_x(chunk0, 3)
    chunk2 = over_x(chunk1, 3)

    me = lax.axis_index("tensor")

    def columns(bits):
        return lax.dynamic_slice_in_dim(out_weight, (me ^ bits) * 1024, 1024, 1)

    cot_chip = to_chip(cot_late)
    cot_diag = to_core(cot_chip)
    w0, part0 = forward(q, [(chunk0,), comp], (False, True), 0.03)
    part0, cot = lax.optimization_barrier((part0, cot))
    cot_core = to_core(cot)
    half = dot_nt(columns(0), cot) + dot_nt(columns(1), cot_core)
    half, chunk1, chunk3 = lax.optimization_barrier((half, chunk1, chunk3))
    w13, part13 = forward(q, [(chunk1,), (chunk3,)], (False, False))
    dout = (half + dot_nt(columns(2), cot_chip) + dot_nt(columns(3), cot_diag)).astype(BF16)
    w2, (alpha0, alpha13, alpha2), delta, mixed = forward_merge(
        lengths, q, dout, [(chunk2,)], [part0, part13]
    )
    (g2,), dq = backward(q, dout, delta, [alpha2], [(chunk2,)], w2, BF16, None, False)

    def partial_out(bits):
        block = lax.dot_general(
            mixed, columns(bits), (((0,), (0,)), ((), ())), preferred_element_type=F32
        )
        return block.astype(BF16)

    other = to_core(jnp.concatenate([partial_out(1), partial_out(3)], axis=0))
    other, dq = lax.optimization_barrier((other, dq))
    pair_mine = partial_out(0).astype(F32) + other[:SLOTS].astype(F32)
    pair_far = partial_out(2).astype(F32) + other[SLOTS:].astype(F32)
    pair_far, alpha13 = lax.optimization_barrier((pair_far.astype(BF16), alpha13))
    far = to_chip(pair_far)
    (g1, g3), dq = backward(
        q, dout, delta, [alpha13, alpha13], [(chunk1,), (chunk3,)], w13, BF16, dq, False
    )
    (g0, gck, gcv), dq = backward(
        q, dout, delta, [alpha0, alpha0], [(chunk0,), comp], w0, F32, dq, True
    )

    back2, far = lax.optimization_barrier((over_x(g2, 2), far))
    back1, back3 = over_x(g1, 1), over_x(g3, 3)
    rows = g0 + back2.astype(F32) + back1.astype(F32) + back3.astype(F32)
    n = own.shape[0]
    sent = rows.astype(BF16)
    shares = [rows[:n]]
    for i, s in enumerate((1, 3, 2)):
        shares.append(over_z(sent[(i + 1) * n : (i + 2) * n], s).astype(F32))
    key_grad = sum(x[:, :HD] for x in shares).astype(BF16)
    value_grad = sum(x[:, HD:] for x in shares).astype(BF16)
    output = (pair_mine + far.astype(F32)).astype(BF16)
    return (
        output[None, None],
        dq[None, None],
        gck[None, None],
        gcv[None, None],
        key_grad[None],
        value_grad[None],
    )


def solution(mesh):
    wide = P("dp", "group", None, "tensor")
    rows = P("dp", "group", "tensor")
    return jax.shard_map(
        per_device,
        mesh=mesh,
        in_specs=(wide, wide, wide, rows, rows, P("tensor", None), wide, P("dp", "group")),
        out_specs=(wide, wide, wide, wide, rows, rows),
        check_vma=False,
    )
```
